512 devices in a mesh: grid: 256 (over z_lo, y, x, core), head: 2 (over z_hi).
Axes of the slice: x: 4, y: 4, z: 16 (z_hi: 2, z_lo: 8; z = z_hi * 8 + z_lo), core: 2. Of those that a mesh axis runs over, the one named last changes fastest.
Arguments:
- node_query: bfloat16 [8192, 1024], P('grid', 'head'), may hold values from -6 to 6
- node_key: bfloat16 [8192, 1024], P('grid', 'head'), may hold values from -6 to 6
- node_value: bfloat16 [8192, 1024], P('grid', 'head'), may hold values from -6 to 6
- out_grad: bfloat16 [8192, 1024], P('grid', 'head'), may hold values from -6 to 6
- tile_mask: int32 [256, 4, 4], P('grid'), may hold values from 0 to 1, as said below
- tile_type: int32 [256, 4, 4], P('grid'), may hold values from 0 to 15
- edge_table: float32 [16, 128], replicated, may hold values from -6 to 6
- edge_proj: float32 [128, 16], replicated, may hold values from -0.5 to 0.5
Outputs:
- attended: bfloat16 [8192, 1024], P('grid', 'head')
- query_grad: float32 [8192, 1024], P('grid', 'head')
- key_grad: float32 [8192, 1024], P('grid', 'head')
- value_grad: float32 [8192, 1024], P('grid', 'head')
- table_grad: float32 [16, 128], replicated
- proj_grad: float32 [128, 16], replicated
The draws below stay inside these ranges and needn't reach their ends.
Inputs may be any that keep to these rules, and one draw needn't show every extreme that they name: `tile_mask`: tile (a, a) of block r * (17) is 1 for every a and r.
All inputs are finite; a program needn't handle non-finite values.
Results may differ from the reference program's by a relative error of at most 0.015.
Values may be sent and summed in bfloat16 or wider, within the bound.
A program may use at most 64 MiB of HBM per device.

```python
import math
import jax
import jax.numpy as jnp
from jax import lax

HEADS = 16
HEAD_DIM = 64
EDGE_DIM = 128
TYPES = 16
TILE = 128
NB = 512
SIDE = 16
TB = 4
NODES = 8192
MODEL_DIM = 1024


def draw_node_query(key, part):
    key = jax.random.fold_in(key, 1)
    full_shape = (NODES, HEADS * HEAD_DIM)
    values = jnp.clip(jax.random.normal(key, full_shape, jnp.float32), -6.0, 6.0)
    return values.astype(jnp.bfloat16)


def draw_node_key(key, part):
    key = jax.random.fold_in(key, 2)
    full_shape = (NODES, HEADS * HEAD_DIM)
    values = jnp.clip(jax.random.normal(key, full_shape, jnp.float32), -6.0, 6.0)
    return values.astype(jnp.bfloat16)


def draw_tile_mask(key, part):
    key = jax.random.fold_in(key, 3)
    mask_shape = (SIDE * SIDE, TB, TB)
    density = jax.random.randint(jax.random.fold_in(key, 1), (SIDE * SIDE, 1, 1), 1, 9)
    rolled = jax.random.randint(jax.random.fold_in(key, 2), mask_shape, 0, 8)
    filled = (rolled < density).astype(jnp.int32)
    block_ids = jnp.arange(SIDE * SIDE, dtype=jnp.int32)[:, None, None]
    tile_rows = jnp.arange(TB, dtype=jnp.int32)[None, :, None]
    tile_cols = jnp.arange(TB, dtype=jnp.int32)[None, None, :]
    forced = (block_ids % (SIDE + 1) == 0) & (tile_rows == tile_cols)
    return jnp.where(forced, 1, filled).astype(jnp.int32)


def with_ends(result, key, least, largest):
    place = [jax.random.randint(jax.random.fold_in(key, axis), (), 0, length) for axis, length in enumerate(result.shape)]
    longest = result.shape.index(max(result.shape))
    neighbour = place[:longest] + [(place[longest] + 1) % result.shape[longest]] + place[longest + 1:]
    return result.at[tuple(place)].set(least).at[tuple(neighbour)].set(largest)


def levels(rng, extent, pieces, low, top_value):
    gain = 1.0
    for dim, parts in pieces:
        steps = jax.random.uniform(jax.random.fold_in(jax.random.fold_in(rng, 6), dim), (parts,), jnp.float32, low / len(pieces), top_value / len(pieces))
        gain = gain * jnp.repeat(jnp.exp(steps), extent[dim] // parts).reshape((-1,) + (1,) * (len(extent) - 1 - dim))
    return gain


def scatter_about(stream_key, dims, scale, most, shards=(), kind=jnp.bfloat16):
    values = scale * jax.random.normal(stream_key, dims, jnp.float32)
    if shards:
        values = values * levels(stream_key, dims, shards, -0.22, 0.18)
    return jnp.clip(values, -most, most).astype(kind)


def setup_inputs(seed: int = 0) -> dict:
    seeds = jax.random.split(jax.random.key(seed), 9)
    node_query = draw_node_query(jax.random.fold_in(seeds[8], 71), 0)
    node_key = draw_node_key(jax.random.fold_in(seeds[8], 71), 0)
    node_value = scatter_about(seeds[2], (NODES, MODEL_DIM), 1.0, 6.0, ((0, 256), (1, 2)))
    out_grad = scatter_about(seeds[3], (NODES, MODEL_DIM), 1.0, 6.0, ((0, 256), (1, 2)))
    tile_mask = draw_tile_mask(jax.random.fold_in(seeds[8], 71), 0)
    tile_type = with_ends(jax.random.randint(seeds[5], (SIDE * SIDE, TB, TB), 0, TYPES), jax.random.fold_in(seeds[5], 1), 0, TYPES - 1).astype(jnp.int32)
    edge_table = scatter_about(seeds[6], (TYPES, EDGE_DIM), 1.0, 6.0, (), jnp.float32)
    edge_proj = scatter_about(seeds[7], (EDGE_DIM, HEADS), EDGE_DIM ** -0.5, 0.5, (), jnp.float32)
    return dict(node_query=node_query, node_key=node_key, node_value=node_value, out_grad=out_grad, tile_mask=tile_mask, tile_type=tile_type, edge_table=edge_table, edge_proj=edge_proj)


neg_fill = -1e+30
highest = lax.Precision.HIGHEST

def expand_tiles(matrix):
    return jnp.repeat(jnp.repeat(matrix, TILE, axis=0), TILE, axis=1)

def spread_blocks(blocks):
    return blocks.reshape(SIDE, SIDE, TB, TB).transpose(0, 2, 1, 3).reshape(SIDE * TB, SIDE * TB)

def join_heads(stacked):
    return stacked.transpose(1, 0, 2).reshape(stacked.shape[1], -1)

def reference(node_query, node_key, node_value, out_grad, tile_mask, tile_type, edge_table, edge_proj):
    score_scale = 1.0 / math.sqrt(HEAD_DIM)
    fwd_mask = spread_blocks(tile_mask)
    fwd_type = spread_blocks(tile_type)
    rev_mask = fwd_mask.T
    rev_type = fwd_type.T
    type_ids = jnp.arange(TYPES, dtype=jnp.int32)
    edge_hot = (fwd_type[:, :, None] == type_ids).astype(jnp.float32) * fwd_mask[:, :, None].astype(jnp.float32)
    edge_hot = edge_hot + (rev_type[:, :, None] == type_ids).astype(jnp.float32) * rev_mask[:, :, None].astype(jnp.float32)
    type_bias = jnp.dot(edge_table, edge_proj, precision=highest)
    tile_bias = jnp.einsum('abt,th->hab', edge_hot, type_bias, precision=highest)
    allowed_tiles = fwd_mask + rev_mask > 0
    key_heads = node_key.reshape(NODES, HEADS, HEAD_DIM).transpose(1, 0, 2)
    value_heads = node_value.reshape(NODES, HEADS, HEAD_DIM).transpose(1, 0, 2)

    def one_group(carry, group):
        key_sum, value_sum, type_grad = carry
        query_rows = lax.dynamic_slice_in_dim(node_query, group * NB, NB, 0)
        grad_rows = lax.dynamic_slice_in_dim(out_grad, group * NB, NB, 0)
        allowed = expand_tiles(lax.dynamic_slice_in_dim(allowed_tiles, group * TB, TB, 0))
        hot_rows = lax.dynamic_slice_in_dim(edge_hot, group * TB, TB, 0)

        def one_head(head):
            query_head = lax.dynamic_slice_in_dim(query_rows, head * HEAD_DIM, HEAD_DIM, 1)
            grad_head = lax.dynamic_slice_in_dim(grad_rows, head * HEAD_DIM, HEAD_DIM, 1)
            key_head = lax.dynamic_index_in_dim(key_heads, head, 0, keepdims=False)
            value_head = lax.dynamic_index_in_dim(value_heads, head, 0, keepdims=False)
            bias_all = lax.dynamic_index_in_dim(tile_bias, head, 0, keepdims=False)
            bias_rows = lax.dynamic_slice_in_dim(bias_all, group * TB, TB, 0)
            scores = jnp.dot(query_head, key_head.T, preferred_element_type=jnp.float32) * score_scale
            scores = scores + expand_tiles(bias_rows)
            scores = jnp.where(allowed, scores, neg_fill)
            row_top = lax.optimization_barrier(jnp.max(scores, axis=1))
            exps = jnp.where(allowed, jnp.exp(scores - row_top[:, None]), 0.0)
            weight_sum = lax.optimization_barrier(jnp.sum(exps, axis=1))
            weighted = jnp.dot(exps.astype(jnp.bfloat16), value_head, preferred_element_type=jnp.float32)
            unrounded = weighted / weight_sum[:, None]
            logsum = row_top + jnp.log(weight_sum)
            delta = lax.optimization_barrier(jnp.sum(grad_head.astype(jnp.float32) * unrounded, axis=1))
            probs = jnp.where(allowed, jnp.exp(scores - logsum[:, None]), 0.0)
            prob_grad = jnp.dot(grad_head, value_head.T, preferred_element_type=jnp.float32)
            score_grad = probs * (prob_grad - delta[:, None])
            probs_low = probs.astype(jnp.bfloat16)
            score_low = score_grad.astype(jnp.bfloat16)
            value_part = jnp.dot(probs_low.T, grad_head, preferred_element_type=jnp.float32)
            query_part = jnp.dot(score_low, key_head, preferred_element_type=jnp.float32) * score_scale
            key_part = jnp.dot(score_low.T, query_head, preferred_element_type=jnp.float32) * score_scale
            tile_sums = score_grad.reshape(TB, TILE, SIDE * TB, TILE).sum(axis=(1, 3))
            return (unrounded, query_part, key_part, value_part, tile_sums)
        unrounded, query_part, key_part, value_part, tile_sums = lax.map(one_head, jnp.arange(HEADS, dtype=jnp.int32))
        type_grad = type_grad + jnp.einsum('hab,abt->th', tile_sums, hot_rows, precision=highest)
        return ((key_sum + key_part, value_sum + value_part, type_grad), (join_heads(unrounded), join_heads(query_part)))
    start_carry = (jnp.zeros((HEADS, NODES, HEAD_DIM), jnp.float32), jnp.zeros((HEADS, NODES, HEAD_DIM), jnp.float32), jnp.zeros((TYPES, HEADS), jnp.float32))
    final_carry, group_outs = lax.scan(one_group, start_carry, jnp.arange(SIDE, dtype=jnp.int32))
    key_sum, value_sum, type_grad = final_carry
    attended = group_outs[0].reshape(NODES, MODEL_DIM).astype(jnp.bfloat16)
    query_grad = group_outs[1].reshape(NODES, MODEL_DIM)
    key_grad = join_heads(key_sum)
    value_grad = join_heads(value_sum)
    table_grad = jnp.dot(type_grad, edge_proj.T, precision=highest)
    proj_grad = jnp.dot(edge_table.T, type_grad, precision=highest)
    return (attended, query_grad, key_grad, value_grad, table_grad, proj_grad)
```

```python
import jax
import jax.numpy as jnp
from jax import lax
from jax.experimental import pallas as pl
from jax.experimental.pallas import tpu as pltpu
from jax.sharding import PartitionSpec as P

F32 = jnp.float32
BF16 = jnp.bfloat16
MESH = pl.DeviceIdType.MESH

NZ, NY, NX, NC = 8, 4, 4, 2
NXC = NX * NC
ROWS = 32
HD = 64
TILE_TYPES = 16
QN = NY * NZ * ROWS
KB = NZ * ROWS
MASKED = -1e30

(G_AQ, G_AK, G_MX, G_MY, G_MZ, G_QD, G_ST, G_O, G_DQ, G_RS, G_TX, G_TY, G_TZ, G_X1, G_X2, G_KV) = range(16)
N_SEMS = 16 + NXC

QCHUNK = 512


def dot_nt(a, b):
    return lax.dot_general(a, b, (((1,), (1,)), ((), ())), preferred_element_type=F32)


def dot_tn(a, b):
    return lax.dot_general(a, b, (((0,), (0,)), ((), ())), preferred_element_type=F32)


def dot_nn(a, b):
    return lax.dot_general(a, b, (((1,), (0,)), ((), ())), preferred_element_type=F32)


def split3(x):
    hi = x.astype(BF16)
    rest = x - hi.astype(F32)
    mid = rest.astype(BF16)
    low = (rest - mid.astype(F32)).astype(BF16)
    return hi, mid, low


def iota(shape, dim):
    return lax.broadcasted_iota(jnp.int32, shape, dim)


def kernel(
    q_ref, k_ref, v_ref, do_ref, mask_ref, type_ref, table_ref, proj_ref,
    att_ref, dq_ref, dk_ref, dv_ref, dtable_ref, dproj_ref,
    stq, stk, qd, kvb, q0, d0, qbias, konehot, expand,
    mx, my, tiles, fsel, gsel, projt, square,
    exps, dprob, tops, stat, out_t, dqt, tsum,
    osend, orecv, dsend, drecv, rsend, rrecv,
    tx, ty, tz, x1s, x1r, x2s, x2r,
    send, recv,
):
    g = lax.axis_index("grid")
    zh = lax.axis_index("head")
    core = g % 2
    x = (g // 2) % 4
    y = (g // 8) % 4
    z = g // 32
    xc = g % 8
    zf = zh * NZ + z

    def dev(z_, y_, xc_, zh_):
        return ((z_ * NY + y_) * NXC + xc_, zh_)

    def put(src, dst, group, where, slot=None):
        pltpu.make_async_remote_copy(
            src_ref=src, dst_ref=dst, send_sem=send.at[group],
            recv_sem=recv.at[group if slot is None else slot],
            device_id=where, device_id_type=MESH,
        ).start()

    def await_bytes(ref, sem):
        pltpu.make_async_copy(ref, ref, sem).wait()

    z_peers = [(z + d) % NZ for d in range(1, NZ)]
    y_peers = [(y + d) % NY for d in range(1, NY)]
    xc_peers = [(xc + d) % NXC for d in range(1, NXC)]
    zf_peers = [(zf + d) % (2 * NZ) for d in range(1, 2 * NZ)]

    barrier = pltpu.get_barrier_semaphore()
    for p in xc_peers:
        pl.semaphore_signal(barrier, inc=1, device_id=dev(z, y, p, zh), device_id_type=MESH)
    for p in y_peers:
        pl.semaphore_signal(barrier, inc=1, device_id=dev(z, p, xc, zh), device_id_type=MESH)
    for p in zf_peers:
        pl.semaphore_signal(barrier, inc=1, device_id=dev(p % NZ, y, xc, p // NZ), device_id_type=MESH)

    row_base = (y // 2) * 4
    lane_base = ((y % 2) * 8 + xc) * 4
    rows8 = iota((8, 128), 0)
    lanes8 = iota((8, 128), 1)
    code = jnp.zeros((8, 128), jnp.int32)
    for a in range(4):
        for b in range(4):
            value = mask_ref[0, a, b] * (type_ref[0, a, b] + 1)
            code = jnp.where((rows8 == row_base + a) & (lanes8 == lane_base + b), value, code)
    mx[xc] = code.astype(F32)

    for h in range(NZ):
        cols = slice(h * HD, (h + 1) * HD)
        scaled = (q_ref[:, cols].astype(F32) * 0.125).astype(BF16)
        stq[h] = jnp.concatenate([scaled, do_ref[:, cols]], axis=1)
        stk[h] = jnp.concatenate([k_ref[:, cols], v_ref[:, cols]], axis=1)

    pl.semaphore_wait(barrier, len(xc_peers) + len(y_peers) + len(zf_peers))

    own_rows = pl.ds(pl.multiple_of(z * ROWS, ROWS), ROWS)
    for p in xc_peers:
        put(mx.at[xc], mx.at[xc], G_MX, dev(z, y, p, zh))
    for p in z_peers:
        put(stk.at[p], kvb.at[xc, own_rows], G_AK, dev(p, y, xc, zh))
        put(stq.at[p], qd.at[y, own_rows], G_AQ, dev(p, y, xc, zh))
    kvb[xc, own_rows] = stk[z]
    qd[y, own_rows] = stq[z]

    square[...] = jnp.zeros((128, 128), F32)
    square[:, 0:16] = proj_ref[...]
    projt[...] = jnp.transpose(square[...])[0:16]
    kn = iota((KB, 128), 1)
    kt = iota((KB, 128), 0) // ROWS
    for par in range(2):
        konehot[par] = jnp.where((kn < 48) & (kn % 16 == 2 * kt + par), 1.0, 0.0).astype(BF16)
    qi = iota((QN, 128), 0)
    q_tile = 8 * ((qi % KB) // ROWS) + 2 * (qi // KB) + x // 2
    expand[...] = jnp.where(iota((QN, 128), 1) == q_tile, 1.0, 0.0).astype(BF16)
    stat[y] = jnp.where(iota((8, QN), 0) == 0, -3e38, 0.0)
    out_t[...] = jnp.zeros_like(out_t)
    dqt[...] = jnp.zeros_like(dqt)
    tsum[...] = jnp.zeros_like(tsum)

    await_bytes(mx.at[pl.ds(0, 7)], recv.at[G_MX])
    total = mx[0]
    for i in range(1, NXC):
        total = total + mx[i]
    my[y] = total
    for p in y_peers:
        put(my.at[y], my.at[y], G_MY, dev(z, p, xc, zh))
    await_bytes(my.at[pl.ds(0, 3)], recv.at[G_MY])
    tiles[z] = my[0] + my[1] + my[2] + my[3]
    for p in z_peers:
        put(tiles.at[z], tiles.at[z], G_MZ, dev(p, y, xc, zh))

    await_bytes(stk.at[pl.ds(0, 7)], recv.at[G_AK])
    for p in xc_peers:
        put(kvb.at[xc], kvb.at[xc], G_KV, dev(z, y, p, zh), slot=16 + xc)
    await_bytes(stq.at[pl.ds(0, 7)], recv.at[G_AQ])
    for p in y_peers:
        put(qd.at[y], qd.at[y], G_QD, dev(z, p, xc, zh))

    await_bytes(tiles.at[pl.ds(0, 7)], recv.at[G_MZ])
    fcode = tiles[...].reshape(64, 128)
    square[0:64] = fcode
    square[64:128] = jnp.zeros((64, 128), F32)
    gcode = jnp.transpose(square[...])[0:64]
    own_proj = projt[pl.ds(zf, 1), :]
    type_bias = jnp.sum(table_ref[...] * own_proj, axis=1, keepdims=True)
    type_bias = jnp.broadcast_to(type_bias, (TILE_TYPES, 128))
    bias = jnp.zeros((64, 128), F32)
    for t in range(TILE_TYPES):
        here = type_bias[t : t + 1, :]
        bias = bias + jnp.where(fcode == t + 1.0, here, 0.0) + jnp.where(gcode == t + 1.0, here, 0.0)
    bias = jnp.where(fcode + gcode > 0.0, bias, MASKED)
    sel_n = iota((128, 128), 1)
    sel_b = sel_n % 16
    column = iota((128, 128), 0) == 8 * (sel_b // 2) + 2 * y + sel_b % 2
    columns = jnp.zeros((64, 128), F32)
    for part, piece in enumerate(split3(bias)):
        pick = jnp.where(column & (sel_n // 16 == part), 1.0, 0.0).astype(BF16)
        columns = columns + dot_nn(piece, pick)
    columns = columns.astype(BF16)
    qbias[...] = dot_nn(expand[:, 0:64], columns).astype(BF16)
    kr = iota((16, 64), 0)
    pick_rows = jnp.where(iota((16, 64), 1) == 8 * (kr % 8) + 2 * y + kr // 8, 1.0, 0.0).astype(BF16)
    fsel[...] = dot_nn(pick_rows, gcode.astype(BF16))
    gsel[...] = dot_nn(pick_rows, fcode.astype(BF16))

    await_bytes(qd.at[pl.ds(0, 3)], recv.at[G_QD])
    low_lanes = jnp.where(iota((1, 128), 1) < HD, 1.0, 0.0)
    both = qd[...].reshape(QN, 128).astype(F32)
    q0[...] = (both * low_lanes).astype(BF16)
    d0[...] = (both * (1.0 - low_lanes)).astype(BF16)

    chunks = [slice(c * QCHUNK, (c + 1) * QCHUNK) for c in range(QN // QCHUNK)]

    def block_at(s):
        i = s // 2
        dx = i + (i // 2) * (5 - 2 * i)
        return ((x + dx) % NX) * 2 + (core + s) % 2

    def forward(s, carry):
        j = block_at(s)

        @pl.when(s > 0)
        def _():
            await_bytes(kvb.at[j], recv.at[16 + j])

        kv = kvb[j]
        wide = jnp.concatenate([kv, konehot[j // 4]], axis=1)
        for cs in chunks:
            scores = dot_nt(wide, jnp.concatenate([q0[cs], qbias[cs]], axis=1))
            dp = dot_nt(kv, d0[cs])
            dprob[j, :, cs] = dp
            old = stat[y, 0:1, cs]
            top = jnp.maximum(old, jnp.max(scores, axis=0, keepdims=True))
            e = jnp.exp(scores - top)
            shrink = jnp.exp(old - top)
            eb = e.astype(BF16)
            exps[j, :, cs] = eb
            stat[y, 0:1, cs] = top
            stat[y, 1:2, cs] = stat[y, 1:2, cs] * shrink + jnp.sum(e, axis=0, keepdims=True)
            stat[y, 2:3, cs] = stat[y, 2:3, cs] * shrink + jnp.sum(e * dp, axis=0, keepdims=True)
            tops[j, 0:1, cs] = top
            out_t[:, cs] = out_t[:, cs] * shrink + dot_tn(kv, eb)
        return carry

    lax.fori_loop(0, NXC, forward, 0)

    for p in y_peers:
        put(stat.at[y], stat.at[y], G_ST, dev(z, p, xc, zh))
    await_bytes(stat.at[pl.ds(0, 3)], recv.at[G_ST])
    top = stat[0, 0:1, :]
    for i in range(1, NY):
        top = jnp.maximum(top, stat[i, 0:1, :])
    weight_sum = jnp.zeros((1, QN), F32)
    delta = jnp.zeros((1, QN), F32)
    for i in range(NY):
        scale = jnp.exp(stat[i, 0:1, :] - top)
        weight_sum = weight_sum + stat[i, 1:2, :] * scale
        delta = delta + stat[i, 2:3, :] * scale
    delta = delta / weight_sum
    logsum = top + jnp.log(weight_sum)
    own_scale = jnp.exp(stat[y, 0:1, :] - top) / weight_sum
    for p in range(NY):
        cs = slice(p * KB, (p + 1) * KB)
        osend[p] = out_t[HD : 2 * HD, cs] * own_scale[:, cs]
    orecv[y] = osend[y]
    for p in y_peers:
        put(osend.at[p], orecv.at[y], G_O, dev(z, p, xc, zh))

    def backward(s, carry):
        j = block_at(NXC - 1 - s)
        kv = kvb[j]
        dkv = jnp.zeros((KB, 128), F32)
        for cs in chunks:
            sigma = jnp.exp(tops[j, 0:1, cs] - logsum[:, cs])
            p = exps[j, :, cs].astype(F32) * sigma
            ds = p * (dprob[j, :, cs] - delta[:, cs])
            pb = p.astype(BF16)
            dsb = ds.astype(BF16)
            dkv = dkv + dot_nn(pb, d0[cs]) + dot_nn(dsb, q0[cs])
            dqt[:, cs] = dqt[:, cs] + dot_tn(kv, dsb)
            tsum[j // 4, :, cs] = tsum[j // 4, :, cs] + jnp.sum(ds.reshape(NZ, ROWS, QCHUNK), axis=1)
        rsend[j] = dkv.astype(BF16)

        @pl.when(s < NXC - 1)
        def _():
            put(rsend.at[j], rrecv.at[xc], G_RS, dev(z, y, j, zh))

        return carry

    lax.fori_loop(0, NXC, backward, 0)
    rrecv[xc] = rsend[xc]

    for p in range(NY):
        dsend[p] = (dqt[0:HD, p * KB : (p + 1) * KB] * 0.125).astype(BF16)
    drecv[y] = dsend[y]
    for p in y_peers:
        put(dsend.at[p], drecv.at[y], G_DQ, dev(z, p, xc, zh))

    sums = jnp.zeros((16, 128), F32)
    for piece in split3(tsum[...].reshape(16, QN)):
        sums = sums + dot_nn(piece, expand[...])
    for t in range(TILE_TYPES):
        hits = jnp.where(fsel[...] == t + 1.0, sums, 0.0) + jnp.where(gsel[...] == t + 1.0, sums, 0.0)
        tx[xc, t : t + 1, :] = jnp.sum(hits, axis=0, keepdims=True)
    for p in xc_peers:
        put(tx.at[xc], tx.at[xc], G_TX, dev(z, y, p, zh))

    await_bytes(rrecv.at[pl.ds(0, 7)], recv.at[G_RS])
    total = rrecv[0].astype(F32)
    for i in range(1, NXC):
        total = total + rrecv[i].astype(F32)
    x2s[...] = total.astype(BF16).reshape(NZ, ROWS, 128)
    for p in z_peers:
        put(x2s.at[p], x2r.at[z], G_X2, dev(p, y, xc, zh))
    x2r[z] = x2s[z]

    await_bytes(orecv.at[pl.ds(0, 3)], recv.at[G_O])
    await_bytes(drecv.at[pl.ds(0, 3)], recv.at[G_DQ])
    att = orecv[0] + orecv[1] + orecv[2] + orecv[3]
    dq = drecv[0].astype(F32) + drecv[1].astype(F32) + drecv[2].astype(F32) + drecv[3].astype(F32)
    pair = jnp.transpose(jnp.concatenate([att, dq], axis=0))
    x1s[...] = pair.astype(BF16).reshape(NZ, ROWS, 128)
    for p in z_peers:
        put(x1s.at[p], x1r.at[z], G_X1, dev(p, y, xc, zh))
    x1r[z] = x1s[z]

    await_bytes(tx.at[pl.ds(0, 7)], recv.at[G_TX])
    total = tx[0]
    for i in range(1, NXC):
        total = total + tx[i]
    ty[y] = total
    for p in y_peers:
        put(ty.at[y], ty.at[y], G_TY, dev(z, p, xc, zh))
    await_bytes(ty.at[pl.ds(0, 3)], recv.at[G_TY])
    total = ty[0] + ty[1] + ty[2] + ty[3]
    tz[zf] = jnp.broadcast_to(jnp.sum(total, axis=1, keepdims=True), (TILE_TYPES, 128))
    for p in zf_peers:
        put(tz.at[zf], tz.at[zf], G_TZ, dev(p % NZ, y, xc, p // NZ))

    await_bytes(x2r.at[pl.ds(0, 7)], recv.at[G_X2])
    for h in range(NZ):
        cols = slice(h * HD, (h + 1) * HD)
        dk_ref[:, cols] = x2r[h][:, 0:HD].astype(F32)
        dv_ref[:, cols] = x2r[h][:, HD : 2 * HD].astype(F32)
    await_bytes(x1r.at[pl.ds(0, 7)], recv.at[G_X1])
    for h in range(NZ):
        cols = slice(h * HD, (h + 1) * HD)
        att_ref[:, cols] = x1r[h][:, 0:HD]
        dq_ref[:, cols] = x1r[h][:, HD : 2 * HD].astype(F32)

    await_bytes(tz.at[pl.ds(0, 15)], recv.at[G_TZ])
    dtable = jnp.zeros((TILE_TYPES, 128), F32)
    square[...] = jnp.zeros((128, 128), F32)
    for h in range(2 * NZ):
        dtable = dtable + tz[h] * projt[h : h + 1, :]
        square[h : h + 1, :] = jnp.sum(tz[h] * table_ref[...], axis=0, keepdims=True)
    dtable_ref[...] = dtable
    dproj_ref[...] = jnp.transpose(square[...])[:, 0:16]

    for ref, group in (
        (stk.at[pl.ds(0, 7)], G_AK), (stq.at[pl.ds(0, 7)], G_AQ), (mx.at[pl.ds(0, 7)], G_MX),
        (my.at[pl.ds(0, 3)], G_MY), (tiles.at[pl.ds(0, 7)], G_MZ), (qd.at[pl.ds(0, 3)], G_QD),
        (kvb.at[pl.ds(0, 7)], G_KV), (stat.at[pl.ds(0, 3)], G_ST), (osend.at[pl.ds(0, 3)], G_O),
        (dsend.at[pl.ds(0, 3)], G_DQ), (rsend.at[pl.ds(0, 7)], G_RS), (tx.at[pl.ds(0, 7)], G_TX),
        (ty.at[pl.ds(0, 3)], G_TY), (tz.at[pl.ds(0, 15)], G_TZ), (x1s.at[pl.ds(0, 7)], G_X1),
        (x2s.at[pl.ds(0, 7)], G_X2),
    ):
        await_bytes(ref, send.at[group])


def per_device(node_query, node_key, node_value, out_grad, tile_mask, tile_type, edge_table, edge_proj):
    vmem = pl.BlockSpec(memory_space=pltpu.VMEM)
    smem = pl.BlockSpec(memory_space=pltpu.SMEM)
    half = (ROWS, NZ * HD)
    return pl.pallas_call(
        kernel,
        out_shape=(
            jax.ShapeDtypeStruct(half, BF16),
            jax.ShapeDtypeStruct(half, F32),
            jax.ShapeDtypeStruct(half, F32),
            jax.ShapeDtypeStruct(half, F32),
            jax.ShapeDtypeStruct((TILE_TYPES, 128), F32),
            jax.ShapeDtypeStruct((128, TILE_TYPES), F32),
        ),
        in_specs=[vmem] * 4 + [smem] * 2 + [vmem] * 2,
        out_specs=(vmem,) * 6,
        scratch_shapes=[
            pltpu.VMEM((NZ, ROWS, 128), BF16),
            pltpu.VMEM((NZ, ROWS, 128), BF16),
            pltpu.VMEM((NY, KB, 128), BF16),
            pltpu.VMEM((NXC, KB, 128), BF16),
            pltpu.VMEM((QN, 128), BF16),
            pltpu.VMEM((QN, 128), BF16),
            pltpu.VMEM((QN, 128), BF16),
            pltpu.VMEM((2, KB, 128), BF16),
            pltpu.VMEM((QN, 128), BF16),
            pltpu.VMEM((NXC, 8, 128), F32),
            pltpu.VMEM((NY, 8, 128), F32),
            pltpu.VMEM((NZ, 8, 128), F32),
            pltpu.VMEM((16, 128), F32),
            pltpu.VMEM((16, 128), F32),
            pltpu.VMEM((16, 128), F32),
            pltpu.VMEM((128, 128), F32),
            pltpu.VMEM((NXC, KB, QN), BF16),
            pltpu.VMEM((NXC, KB, QN), F32),
            pltpu.VMEM((NXC, 8, QN), F32),
            pltpu.VMEM((NY, 8, QN), F32),
            pltpu.VMEM((128, QN), F32),
            pltpu.VMEM((128, QN), F32),
            pltpu.VMEM((2, NZ, QN), F32),
            pltpu.VMEM((NY, HD, KB), F32),
            pltpu.VMEM((NY, HD, KB), F32),
            pltpu.VMEM((NY, HD, KB), BF16),
            pltpu.VMEM((NY, HD, KB), BF16),
            pltpu.VMEM((NXC, KB, 128), BF16),
            pltpu.VMEM((NXC, KB, 128), BF16),
            pltpu.VMEM((NXC, TILE_TYPES, 128), F32),
            pltpu.VMEM((NY, TILE_TYPES, 128), F32),
            pltpu.VMEM((2 * NZ, TILE_TYPES, 128), F32),
            pltpu.VMEM((NZ, ROWS, 128), BF16),
            pltpu.VMEM((NZ, ROWS, 128), BF16),
            pltpu.VMEM((NZ, ROWS, 128), BF16),
            pltpu.VMEM((NZ, ROWS, 128), BF16),
            pltpu.SemaphoreType.DMA((16,)),
            pltpu.SemaphoreType.DMA((N_SEMS,)),
        ],
        compiler_params=pltpu.CompilerParams(
            collective_id=0, has_side_effects=True, vmem_limit_bytes=56 * 1024 * 1024
        ),
        cost_estimate=pl.CostEstimate(
            flops=12 * QN * NXC * KB * 128, bytes_accessed=600_000, transcendentals=QN * NXC * KB
        ),
    )(node_query, node_key, node_value, out_grad, tile_mask, tile_type, edge_table, edge_proj)


def solution(mesh):
    split = P("grid", "head")
    return jax.shard_map(
        per_device,
        mesh=mesh,
        in_specs=(split, split, split, split, P("grid", None, None), P("grid", None, None), P(), P()),
        out_specs=(split, split, split, split, P(), P()),
        check_vma=False,
    )
```

```python
import jax
import jax.numpy as jnp
from jax import lax
from jax.experimental import pallas as pl
from jax.experimental.pallas import tpu as pltpu
from jax.sharding import PartitionSpec as P

F32 = jnp.float32
BF16 = jnp.bfloat16
MESH = pl.DeviceIdType.MESH

NZ, NY, NX, NC = 8, 4, 4, 2
NXC = NX * NC
ROWS = 32
HALF = ROWS // 2
HD = 64
TYPES = 16
QN = NY * NZ * ROWS
KB = NZ * ROWS
MASKED = -1e30
QCHUNK = 256
CHUNKS = [slice(c * QCHUNK, (c + 1) * QCHUNK) for c in range(QN // QCHUNK)]
FAR_FIRST = (2, 3, 1, 0)

(G_AQ, G_AK, G_MZ, G_MX, G_MY, G_QD, G_ST, G_O, G_DQ, G_RS, G_TX, G_TY, G_TZ, G_X0, G_X1, G_X2, G_KV, G_PR) = range(18)
S_KV = 18
S_PR = S_KV + NXC
N_SEMS = S_PR + NX


def dot_nt(a, b):
    return lax.dot_general(a, b, (((1,), (1,)), ((), ())), preferred_element_type=F32)


def dot_nn(a, b):
    return lax.dot_general(a, b, (((1,), (0,)), ((), ())), preferred_element_type=F32)


def split3(x):
    hi = x.astype(BF16)
    rest = x - hi.astype(F32)
    mid = rest.astype(BF16)
    low = (rest - mid.astype(F32)).astype(BF16)
    return hi, mid, low


def iota(shape, dim):
    return lax.broadcasted_iota(jnp.int32, shape, dim)


def one_hot(condition):
    return jnp.where(condition, 1.0, 0.0).astype(BF16)


def fold(row):
    return jnp.concatenate([row[:, i * 128 : (i + 1) * 128] for i in range(QN // 128)], axis=0)


def unfold(square):
    return jnp.concatenate([square[i : i + 1, :] for i in range(QN // 128)], axis=1)


def half_rows(full):
    full = full.reshape(NZ, ROWS, HD)
    return jnp.concatenate([full[:, 0:HALF], full[:, HALF:ROWS]], axis=2).astype(BF16)


def kernel(
    q_ref, k_ref, v_ref, do_ref, mask_ref, type_ref, table_ref, projt_ref,
    x0_ref, x1_ref, x2_ref, tg_ref,
    stq, stk, qd, kvb, q0, d0, qt, dt, konehot, expand,
    mz, mx, my, fsel, gsel, square,
    sbuf, dbuf, exps, dprob, tops, stat, packed, out_t, dqt, tsum,
    osend, orecv, dsend, drecv, psend, precv, rsend, rrecv,
    tx, ty, tz, x0s, x0r, x1s, x1r, x2s, x2r,
    send, recv,
):
    g = lax.axis_index("grid")
    zh = lax.axis_index("head")
    core = g % 2
    x = (g // 2) % 4
    y = (g // 8) % 4
    z = g // 32
    xc = g % 8
    zf = zh * NZ + z

    def dev(z_, y_, xc_, zh_):
        return ((z_ * NY + y_) * NXC + xc_, zh_)

    def put(src, dst, group, where, slot=None):
        pltpu.make_async_remote_copy(
            src_ref=src, dst_ref=dst, send_sem=send.at[group],
            recv_sem=recv.at[group if slot is None else slot],
            device_id=where, device_id_type=MESH,
        ).start()

    def await_bytes(ref, sem):
        pltpu.make_async_copy(ref, ref, sem).wait()

    z_peers = [(z + d) % NZ for d in range(1, NZ)]
    y_peers = [(y + d) % NY for d in range(1, NY)]
    x_peers = [(x + d) % NX for d in range(1, NX)]
    xc_peers = [(xc + d) % NXC for d in range(1, NXC)]
    zf_peers = [(zf + d) % (2 * NZ) for d in range(1, 2 * NZ)]

    barrier = pltpu.get_barrier_semaphore()
    for p in zf_peers:
        pl.semaphore_signal(barrier, inc=1, device_id=dev(p % NZ, y, xc, p // NZ), device_id_type=MESH)
    for p in y_peers:
        pl.semaphore_signal(barrier, inc=1, device_id=dev(z, p, xc, zh), device_id_type=MESH)
    for p in xc_peers:
        pl.semaphore_signal(barrier, inc=1, device_id=dev(z, y, p, zh), device_id_type=MESH)

    lanes = iota((1, 128), 1)
    code = jnp.zeros((1, 128), jnp.int32)
    for a in range(4):
        for b in range(4):
            value = mask_ref[0, a, b] * (type_ref[0, a, b] + 1)
            code = jnp.where(lanes == z * 16 + (a * 4 + b), value, code)
    mz[z] = code.astype(F32)

    for h in range(NZ):
        cols = slice(h * HD, (h + 1) * HD)
        scaled = (q_ref[:, cols].astype(F32) * 0.125).astype(BF16)
        stq[h] = jnp.concatenate([scaled, do_ref[:, cols]], axis=1)
        stk[h] = jnp.concatenate([k_ref[:, cols], v_ref[:, cols]], axis=1)

    pl.semaphore_wait(barrier, len(xc_peers) + len(y_peers) + len(zf_peers))

    own_rows = pl.ds(pl.multiple_of(z * ROWS, ROWS), ROWS)
    for p in z_peers:
        put(mz.at[z], mz.at[z], G_MZ, dev(p, y, xc, zh))
    for p in z_peers:
        put(stk.at[p], kvb.at[xc, own_rows], G_AK, dev(p, y, xc, zh))
        put(stq.at[p], qd.at[y, own_rows], G_AQ, dev(p, y, xc, zh))
    kvb[xc, own_rows] = stk[z]
    qd[y, own_rows] = stq[z]

    kn = iota((KB, 128), 1)
    kt = iota((KB, 128), 0) // ROWS
    for par in range(2):
        konehot[par] = one_hot((kn < 48) & (kn % 16 == 2 * kt + par))
    qi = iota((QN, 128), 0)
    q_tile = 8 * ((qi % KB) // ROWS) + 2 * (qi // KB) + x // 2
    expand[...] = one_hot(iota((QN, 128), 1) == q_tile)
    stat[...] = jnp.where(iota((8, QN), 0) == 0, -3e38, 0.0)
    out_t[...] = jnp.zeros_like(out_t)
    dqt[...] = jnp.zeros_like(dqt)
    tsum[...] = jnp.zeros_like(tsum)
    square[...] = jnp.zeros((128, 128), F32)

    await_bytes(mz.at[pl.ds(0, 7)], recv.at[G_MZ])
    total = mz[0]
    for i in range(1, NZ):
        total = total + mz[i]
    mx[xc] = total
    for p in xc_peers:
        put(mx.at[xc], mx.at[xc], G_MX, dev(z, y, p, zh))

    await_bytes(mx.at[pl.ds(0, 7)], recv.at[G_MX])
    my[y] = jnp.concatenate([mx[i] for i in range(NXC)], axis=0)
    for p in y_peers:
        put(my.at[y], my.at[y], G_MY, dev(z, p, xc, zh))

    await_bytes(stk.at[pl.ds(0, 7)], recv.at[G_AK])
    for d in (1, 2, 6, 3, 7, 4, 5):
        p = ((x + d // 2) % NX) * 2 + (core + d) % 2
        put(kvb.at[xc], kvb.at[xc], G_KV, dev(z, y, p, zh), slot=S_KV + xc)
    await_bytes(stq.at[pl.ds(0, 7)], recv.at[G_AQ])
    for p in y_peers:
        put(qd.at[y], qd.at[y], G_QD, dev(z, p, xc, zh))

    await_bytes(my.at[pl.ds(0, 3)], recv.at[G_MY])
    codes = my[...].reshape(NY * NXC, 128).astype(BF16)
    pick_b, pick_a = iota((256, 128), 0) // 64, iota((256, 128), 0) % 64
    picked = dot_nt(one_hot(iota((256, 128), 1) == (pick_a // 8) * 16 + (pick_a % 4) * 4 + pick_b), codes)
    same_half = (iota((256, 32), 0) // 4) % 2 == iota((256, 32), 1) // 16
    picked = jnp.where(same_half, picked, 0.0).astype(BF16)
    fcode = jnp.zeros((64, 128), F32)
    for b in range(4):
        spread = one_hot(iota((32, 128), 1) == 4 * (iota((32, 128), 0) % 16) + b)
        fcode = fcode + dot_nn(picked[b * 64 : (b + 1) * 64], spread)
    square[0:64] = fcode
    gcode = jnp.transpose(square[...])[0:64]
    own_proj = projt_ref[pl.ds(zf, 1), :]
    type_bias = jnp.sum(table_ref[...] * own_proj, axis=1, keepdims=True)
    type_bias = jnp.broadcast_to(type_bias, (TYPES, 128))
    bias = jnp.zeros((64, 128), F32)
    for t in range(TYPES):
        here = type_bias[t : t + 1, :]
        bias = bias + jnp.where(fcode == t + 1.0, here, 0.0) + jnp.where(gcode == t + 1.0, here, 0.0)
    bias = jnp.where(fcode + gcode > 0.0, bias, MASKED)
    sel_n = iota((128, 128), 1)
    sel_b = sel_n % 16
    column = iota((128, 128), 0) == 8 * (sel_b // 2) + 2 * y + sel_b % 2
    columns = jnp.zeros((64, 128), F32)
    for part, piece in enumerate(split3(bias)):
        columns = columns + dot_nn(piece, one_hot(column & (sel_n // 16 == part)))
    columns = columns.astype(BF16)
    qt[128:256, :] = jnp.transpose(dot_nn(expand[:, 0:64], columns)).astype(BF16)
    kr = iota((16, 64), 0)
    pick_rows = one_hot(iota((16, 64), 1) == 8 * (kr % 8) + 2 * y + kr // 8)
    fsel[...] = dot_nn(pick_rows, gcode.astype(BF16))
    gsel[...] = dot_nn(pick_rows, fcode.astype(BF16))

    await_bytes(qd.at[pl.ds(0, 3)], recv.at[G_QD])
    low_lanes = jnp.where(lanes < HD, 1.0, 0.0)
    both = qd[...].reshape(QN, 128).astype(F32)
    q_only = both * low_lanes
    d_only = both * (1.0 - low_lanes)
    q0[...] = q_only.astype(BF16)
    d0[...] = d_only.astype(BF16)
    qt[0:128, :] = jnp.transpose(q_only).astype(BF16)
    dt[...] = jnp.transpose(d_only).astype(BF16)

    def block_at(i, c):
        return ((x + i) % NX) * 2 + (core + c) % 2

    order = [block_at(i, c) for i in reversed(FAR_FIRST) for c in range(NC)]

    def products(s):
        j = order[s]
        if s > 0:
            await_bytes(kvb.at[j], recv.at[S_KV + j])
        kv = kvb[j]
        sbuf[s % 2] = dot_nn(jnp.concatenate([kv, konehot[j // 4]], axis=1), qt[...])
        dbuf[s % 2] = dot_nn(kv, dt[...])

    def forward(s):
        j = order[s]
        kvt = jnp.transpose(kvb[j])
        for cs in CHUNKS:
            scores = sbuf[s % 2, :, cs]
            dp = dbuf[s % 2, :, cs]
            dprob[j, :, cs] = dp
            old = stat[0:1, cs]
            top = jnp.maximum(old, jnp.max(scores, axis=0, keepdims=True))
            e = jnp.exp(scores - top)
            shrink = jnp.exp(old - top)
            eb = e.astype(BF16)
            exps[j, :, cs] = eb
            stat[0:1, cs] = top
            stat[1:2, cs] = stat[1:2, cs] * shrink + jnp.sum(e, axis=0, keepdims=True)
            stat[2:3, cs] = stat[2:3, cs] * shrink + jnp.sum(e * dp, axis=0, keepdims=True)
            tops[j, 0:1, cs] = top
            out_t[:, cs] = out_t[:, cs] * shrink + dot_nn(kvt, eb)

    products(0)
    for s in range(NXC):
        if s + 1 < NXC:
            products(s + 1)
        forward(s)

    for i in range(3):
        packed[y, i] = fold(stat[i : i + 1, :])
    for p in y_peers:
        put(packed.at[y], packed.at[y], G_ST, dev(z, p, xc, zh))
    await_bytes(packed.at[pl.ds(0, 3)], recv.at[G_ST])
    top = packed[0, 0]
    for i in range(1, NY):
        top = jnp.maximum(top, packed[i, 0])
    weight_sum = jnp.zeros((8, 128), F32)
    delta = jnp.zeros((8, 128), F32)
    for i in range(NY):
        scale = jnp.exp(packed[i, 0] - top)
        weight_sum = weight_sum + packed[i, 1] * scale
        delta = delta + packed[i, 2] * scale
    delta = unfold(delta / weight_sum)
    logsum = unfold(top + jnp.log(weight_sum))
    own_scale = unfold(jnp.exp(packed[y, 0] - top) / weight_sum)
    for p in range(NY):
        cs = slice(p * KB, (p + 1) * KB)
        osend[p] = out_t[HD : 2 * HD, cs] * own_scale[:, cs]
    orecv[y] = osend[y]
    for p in y_peers:
        put(osend.at[p], orecv.at[y], G_O, dev(z, p, xc, zh))

    def backward(j):
        kv = kvb[j]
        kvt = jnp.transpose(kv)
        dkv = jnp.zeros((KB, 128), F32)
        for cs in CHUNKS:
            sigma = jnp.exp(tops[j, 0:1, cs] - logsum[:, cs])
            p = exps[j, :, cs].astype(F32) * sigma
            ds = p * (dprob[j, :, cs] - delta[:, cs])
            pb = p.astype(BF16)
            dsb = ds.astype(BF16)
            dkv = dkv + dot_nn(pb, d0[cs]) + dot_nn(dsb, q0[cs])
            dqt[:, cs] = dqt[:, cs] + dot_nn(kvt, dsb)
            tsum[j // 4, :, cs] = tsum[j // 4, :, cs] + jnp.sum(ds.reshape(NZ, ROWS, QCHUNK), axis=1)
        return dkv

    other = (core + 1) % 2

    def add_partner(n, dkv):
        await_bytes(precv.at[n], recv.at[S_PR + n])
        return dkv + precv[n].astype(F32)

    waiting = None
    for n, i in enumerate(FAR_FIRST):
        psend[n] = backward(block_at(i, 1)).astype(BF16)
        put(psend.at[n], precv.at[n], G_PR, dev(z, y, x * 2 + other, zh), slot=S_PR + n)
        if waiting is not None:
            rsend[n - 1] = add_partner(n - 1, waiting).astype(BF16)
            put(rsend.at[n - 1], rrecv.at[x], G_RS, dev(z, y, block_at(FAR_FIRST[n - 1], 0), zh))
        if n == 3:
            await_bytes(orecv.at[pl.ds(0, 3)], recv.at[G_O])
            att = orecv[0] + orecv[1] + orecv[2] + orecv[3]
            x0s[...] = half_rows(jnp.transpose(att))
            for p in z_peers:
                put(x0s.at[p], x0r.at[z], G_X0, dev(p, y, xc, zh))
            x0r[z] = x0s[z]
        waiting = backward(block_at(i, 0))

    for p in range(NY):
        dsend[p] = (dqt[0:HD, p * KB : (p + 1) * KB] * 0.125).astype(BF16)
    drecv[y] = dsend[y]
    for p in y_peers:
        put(dsend.at[p], drecv.at[y], G_DQ, dev(z, p, xc, zh))

    sums = jnp.zeros((16, 128), F32)
    for piece in split3(tsum[...].reshape(16, QN)):
        sums = sums + dot_nn(piece, expand[...])
    for t in range(TYPES):
        hits = jnp.where(fsel[...] == t + 1.0, sums, 0.0) + jnp.where(gsel[...] == t + 1.0, sums, 0.0)
        square[t : t + 1, :] = jnp.sum(hits, axis=0, keepdims=True)
    square[TYPES:64, :] = jnp.zeros((64 - TYPES, 128), F32)
    tx[xc] = jnp.sum(jnp.transpose(square[...]), axis=0, keepdims=True)
    for p in xc_peers:
        put(tx.at[xc], tx.at[xc], G_TX, dev(z, y, p, zh))

    own = add_partner(3, waiting)
    await_bytes(rrecv.at[pl.ds(0, 3)], recv.at[G_RS])
    for i in (1, 2, 3):
        own = own + rrecv[(x + i) % NX].astype(F32)
    x2s[...] = own.astype(BF16).reshape(NZ, ROWS, 128)
    for p in z_peers:
        put(x2s.at[p], x2r.at[z], G_X2, dev(p, y, xc, zh))
    x2r[z] = x2s[z]

    await_bytes(tx.at[pl.ds(0, 7)], recv.at[G_TX])
    total = tx[0]
    for i in range(1, NXC):
        total = total + tx[i]
    ty[y] = total
    for p in y_peers:
        put(ty.at[y], ty.at[y], G_TY, dev(z, p, xc, zh))

    await_bytes(drecv.at[pl.ds(0, 3)], recv.at[G_DQ])
    dq = drecv[0].astype(F32) + drecv[1].astype(F32) + drecv[2].astype(F32) + drecv[3].astype(F32)
    x1s[...] = half_rows(jnp.transpose(dq))
    for p in z_peers:
        put(x1s.at[p], x1r.at[z], G_X1, dev(p, y, xc, zh))
    x1r[z] = x1s[z]

    await_bytes(ty.at[pl.ds(0, 3)], recv.at[G_TY])
    tz[zf] = ty[0] + ty[1] + ty[2] + ty[3]
    for p in zf_peers:
        put(tz.at[zf], tz.at[zf], G_TZ, dev(p % NZ, y, xc, p // NZ))

    for ref, group in (
        (stk.at[pl.ds(0, 7)], G_AK), (stq.at[pl.ds(0, 7)], G_AQ), (mz.at[pl.ds(0, 7)], G_MZ),
        (mx.at[pl.ds(0, 7)], G_MX), (my.at[pl.ds(0, 3)], G_MY), (qd.at[pl.ds(0, 3)], G_QD),
        (kvb.at[pl.ds(0, 7)], G_KV), (packed.at[pl.ds(0, 3)], G_ST), (osend.at[pl.ds(0, 3)], G_O),
        (psend.at[pl.ds(0, 4)], G_PR), (dsend.at[pl.ds(0, 3)], G_DQ), (rsend.at[pl.ds(0, 3)], G_RS),
        (tx.at[pl.ds(0, 7)], G_TX), (ty.at[pl.ds(0, 3)], G_TY), (x0s.at[pl.ds(0, 7)], G_X0),
        (x2s.at[pl.ds(0, 7)], G_X2), (x1s.at[pl.ds(0, 7)], G_X1), (tz.at[pl.ds(0, 15)], G_TZ),
    ):
        await_bytes(ref, send.at[group])

    await_bytes(x0r.at[pl.ds(0, 7)], recv.at[G_X0])
    x0_ref[...] = x0r[...]
    await_bytes(x2r.at[pl.ds(0, 7)], recv.at[G_X2])
    x2_ref[...] = x2r[...]
    await_bytes(x1r.at[pl.ds(0, 7)], recv.at[G_X1])
    x1_ref[...] = x1r[...]
    await_bytes(tz.at[pl.ds(0, 15)], recv.at[G_TZ])
    tg_ref[...] = jnp.concatenate([tz[h] for h in range(2 * NZ)], axis=0)


def lay_out(
    x0_ref, x1_ref, x2_ref, tg_ref, table_ref, projt_ref,
    att_ref, dq_ref, dk_ref, dv_ref, dtable_ref, dprojt_ref, square,
):
    low, high = slice(0, HD), slice(HD, 2 * HD)
    for h in range(NZ):
        cols = slice(h * HD, (h + 1) * HD)
        att_ref[0:HALF, cols] = x0_ref[h][:, low]
        att_ref[HALF:ROWS, cols] = x0_ref[h][:, high]
        dq_ref[0:HALF, cols] = x1_ref[h][:, low].astype(F32)
        dq_ref[HALF:ROWS, cols] = x1_ref[h][:, high].astype(F32)
        dk_ref[:, cols] = x2_ref[h][:, low].astype(F32)
        dv_ref[:, cols] = x2_ref[h][:, high].astype(F32)
    tg = tg_ref[...]
    square[...] = jnp.zeros((128, 128), F32)
    square[0:16] = tg
    tg_t = jnp.transpose(square[...])
    dtable = jnp.zeros((TYPES, 128), F32)
    dprojt = jnp.zeros((2 * NZ, 128), F32)
    for i in range(16):
        dtable = dtable + tg_t[0:16, i : i + 1] * projt_ref[i : i + 1, :]
        dprojt = dprojt + tg[:, i : i + 1] * table_ref[i : i + 1, :]
    dtable_ref[...] = dtable
    dprojt_ref[...] = dprojt


def per_device(node_query, node_key, node_value, out_grad, tile_mask, tile_type, edge_table, edge_proj):
    vmem = pl.BlockSpec(memory_space=pltpu.VMEM)
    smem = pl.BlockSpec(memory_space=pltpu.SMEM)
    half = (ROWS, NZ * HD)
    proj_t = edge_proj.T
    spread = pl.pallas_call(
        kernel,
        out_shape=(
            jax.ShapeDtypeStruct((NZ, HALF, 128), BF16),
            jax.ShapeDtypeStruct((NZ, HALF, 128), BF16),
            jax.ShapeDtypeStruct((NZ, ROWS, 128), BF16),
            jax.ShapeDtypeStruct((2 * NZ, 128), F32),
        ),
        in_specs=[vmem] * 4 + [smem] * 2 + [vmem] * 2,
        out_specs=(vmem,) * 4,
        scratch_shapes=[
            pltpu.VMEM((NZ, ROWS, 128), BF16),
            pltpu.VMEM((NZ, ROWS, 128), BF16),
            pltpu.VMEM((NY, KB, 128), BF16),
            pltpu.VMEM((NXC, KB, 128), BF16),
            pltpu.VMEM((QN, 128), BF16),
            pltpu.VMEM((QN, 128), BF16),
            pltpu.VMEM((256, QN), BF16),
            pltpu.VMEM((128, QN), BF16),
            pltpu.VMEM((2, KB, 128), BF16),
            pltpu.VMEM((QN, 128), BF16),
            pltpu.VMEM((NZ, 1, 128), F32),
            pltpu.VMEM((NXC, 1, 128), F32),
            pltpu.VMEM((NY, NXC, 128), F32),
            pltpu.VMEM((16, 128), F32),
            pltpu.VMEM((16, 128), F32),
            pltpu.VMEM((128, 128), F32),
            pltpu.VMEM((2, KB, QN), F32),
            pltpu.VMEM((2, KB, QN), F32),
            pltpu.VMEM((NXC, KB, QN), BF16),
            pltpu.VMEM((NXC, KB, QN), F32),
            pltpu.VMEM((NXC, 8, QN), F32),
            pltpu.VMEM((8, QN), F32),
            pltpu.VMEM((NY, 3, 8, 128), F32),
            pltpu.VMEM((128, QN), F32),
            pltpu.VMEM((128, QN), F32),
            pltpu.VMEM((2, NZ, QN), F32),
            pltpu.VMEM((NY, HD, KB), F32),
            pltpu.VMEM((NY, HD, KB), F32),
            pltpu.VMEM((NY, HD, KB), BF16),
            pltpu.VMEM((NY, HD, KB), BF16),
            pltpu.VMEM((NX, KB, 128), BF16),
            pltpu.VMEM((NX, KB, 128), BF16),
            pltpu.VMEM((NX, KB, 128), BF16),
            pltpu.VMEM((NX, KB, 128), BF16),
            pltpu.VMEM((NXC, 1, 128), F32),
            pltpu.VMEM((NY, 1, 128), F32),
            pltpu.VMEM((2 * NZ, 1, 128), F32),
            pltpu.VMEM((NZ, HALF, 128), BF16),
            pltpu.VMEM((NZ, HALF, 128), BF16),
            pltpu.VMEM((NZ, HALF, 128), BF16),
            pltpu.VMEM((NZ, HALF, 128), BF16),
            pltpu.VMEM((NZ, ROWS, 128), BF16),
            pltpu.VMEM((NZ, ROWS, 128), BF16),
            pltpu.SemaphoreType.DMA((18,)),
            pltpu.SemaphoreType.DMA((N_SEMS,)),
        ],
        compiler_params=pltpu.CompilerParams(
            collective_id=0, has_side_effects=True, vmem_limit_bytes=56 * 1024 * 1024
        ),
        cost_estimate=pl.CostEstimate(
            flops=12 * QN * NXC * KB * 128, bytes_accessed=600_000, transcendentals=QN * NXC * KB
        ),
    )(node_query, node_key, node_value, out_grad, tile_mask, tile_type, edge_table, proj_t)
    att, dq, dk, dv, dtable, dprojt = pl.pallas_call(
        lay_out,
        out_shape=(
            jax.ShapeDtypeStruct(half, BF16),
            jax.ShapeDtypeStruct(half, F32),
            jax.ShapeDtypeStruct(half, F32),
            jax.ShapeDtypeStruct(half, F32),
            jax.ShapeDtypeStruct((TYPES, 128), F32),
            jax.ShapeDtypeStruct((2 * NZ, 128), F32),
        ),
        in_specs=[vmem] * 6,
        out_specs=(vmem,) * 6,
        scratch_shapes=[pltpu.VMEM((128, 128), F32)],
    )(*spread, edge_table, proj_t)
    return att, dq, dk, dv, dtable, dprojt.T


def solution(mesh):
    split = P("grid", "head")
    return jax.shard_map(
        per_device,
        mesh=mesh,
        in_specs=(split, split, split, split, P("grid", None, None), P("grid", None, None), P(), P()),
        out_specs=(split, split, split, split, P(), P()),
        check_vma=False,
    )
```

```python
import jax
import jax.numpy as jnp
from jax import lax
from jax.experimental import pallas as pl
from jax.experimental.pallas import tpu as pltpu
from jax.sharding import PartitionSpec as P

F32 = jnp.float32
BF16 = jnp.bfloat16
MESH = pl.DeviceIdType.MESH

NZ, NY, NX, NC = 8, 4, 4, 2
NXC = NX * NC
PLANE = NY * NXC
ROWS = 32
HALF = ROWS // 2
HD = 64
TYPES = 16
QN = NY * NZ * ROWS
KB = NZ * ROWS
MASKED = -1e30
QCHUNK = 256
CHUNKS = [slice(c * QCHUNK, (c + 1) * QCHUNK) for c in range(QN // QCHUNK)]
FAR_FIRST = (2, 3, 1, 0)

(G_AQ, G_AK, G_MZ, G_MX, G_QD, G_ST, G_O, G_DQ, G_RS, G_TX, G_TZ, G_X0, G_X1, G_X2, G_KV, G_PR) = range(16)
S_KV = 16
S_PR = S_KV + NXC
N_SEMS = S_PR + NX


def dot_nt(a, b):
    return lax.dot_general(a, b, (((1,), (1,)), ((), ())), preferred_element_type=F32)


def dot_nn(a, b):
    return lax.dot_general(a, b, (((1,), (0,)), ((), ())), preferred_element_type=F32)


def split3(x):
    hi = x.astype(BF16)
    rest = x - hi.astype(F32)
    mid = rest.astype(BF16)
    low = (rest - mid.astype(F32)).astype(BF16)
    return hi, mid, low


def iota(shape, dim):
    return lax.broadcasted_iota(jnp.int32, shape, dim)


def one_hot(condition):
    return jnp.where(condition, 1.0, 0.0).astype(BF16)


def fold(row):
    return jnp.concatenate([row[:, i * 128 : (i + 1) * 128] for i in range(QN // 128)], axis=0)


def unfold(square):
    return jnp.concatenate([square[i : i + 1, :] for i in range(QN // 128)], axis=1)


def half_rows(full):
    full = full.reshape(NZ, ROWS, HD)
    return jnp.concatenate([full[:, 0:HALF], full[:, HALF:ROWS]], axis=2).astype(BF16)


def kernel(
    q_ref, k_ref, v_ref, do_ref, mask_ref, type_ref, table_ref, projt_ref,
    x0_ref, x1_ref, x2_ref, tg_ref,
    stq, stk, qd, kvb, q0, d0, qt, dt, konehot, expand,
    mz, mx, fsel, gsel, square,
    sbuf, dbuf, exps, dprob, tops, stat, packed, out_t, dqt, tsum,
    osend, orecv, dsend, drecv, psend, precv, rsend, rrecv,
    tx, tz, x0s, x0r, x1s, x1r, x2s, x2r,
    send, recv,
):
    g = lax.axis_index("grid")
    zh = lax.axis_index("head")
    core = g % 2
    x = (g // 2) % 4
    y = (g // 8) % 4
    z = g // 32
    xc = g % 8
    n_plane = g % PLANE
    zf = zh * NZ + z

    def dev(z_, y_, xc_, zh_):
        return ((z_ * NY + y_) * NXC + xc_, zh_)

    def put(src, dst, group, where, slot=None):
        pltpu.make_async_remote_copy(
            src_ref=src, dst_ref=dst, send_sem=send.at[group],
            recv_sem=recv.at[group if slot is None else slot],
            device_id=where, device_id_type=MESH,
        ).start()

    def await_bytes(ref, sem):
        pltpu.make_async_copy(ref, ref, sem).wait()

    def in_plane(d):
        return (z * PLANE + (n_plane + d) % PLANE, zh)

    def to_plane(slots, group):
        def step(d, carry):
            put(slots.at[n_plane], slots.at[n_plane], group, in_plane(d))
            return carry

        lax.fori_loop(1, PLANE, step, 0)

    def each(count, me):
        def run(act):
            def step(d, carry):
                act((me + d) % count)
                return carry

            lax.fori_loop(1, count, step, 0)

        return run

    barrier = pltpu.get_barrier_semaphore()

    @each(2 * NZ, zf)
    def _(p):
        pl.semaphore_signal(barrier, inc=1, device_id=dev(p % NZ, y, xc, p // NZ), device_id_type=MESH)

    def greet(d, carry):
        pl.semaphore_signal(barrier, inc=1, device_id=in_plane(d), device_id_type=MESH)
        return carry

    lax.fori_loop(1, PLANE, greet, 0)

    lanes = iota((1, 128), 1)
    code = jnp.zeros((1, 128), jnp.int32)
    for a in range(4):
        for b in range(4):
            value = mask_ref[0, a, b] * (type_ref[0, a, b] + 1)
            code = jnp.where(lanes == z * 16 + (a * 4 + b), value, code)
    mz[z] = code.astype(F32)

    for h in range(NZ):
        cols = slice(h * HD, (h + 1) * HD)
        scaled = (q_ref[:, cols].astype(F32) * 0.125).astype(BF16)
        stq[h] = jnp.concatenate([scaled, do_ref[:, cols]], axis=1)
        stk[h] = jnp.concatenate([k_ref[:, cols], v_ref[:, cols]], axis=1)

    pl.semaphore_wait(barrier, PLANE - 1 + 2 * NZ - 1)

    own_rows = pl.ds(pl.multiple_of(z * ROWS, ROWS), ROWS)

    @each(NZ, z)
    def _(p):
        put(mz.at[z], mz.at[z], G_MZ, dev(p, y, xc, zh))

    @each(NZ, z)
    def _(p):
        put(stk.at[p], kvb.at[xc, own_rows], G_AK, dev(p, y, xc, zh))
        put(stq.at[p], qd.at[y, own_rows], G_AQ, dev(p, y, xc, zh))

    kvb[xc, own_rows] = stk[z]
    qd[y, own_rows] = stq[z]

    kn = iota((KB, 128), 1)
    kt = iota((KB, 128), 0) // ROWS
    for par in range(2):
        konehot[par] = one_hot((kn < 48) & (kn % 16 == 2 * kt + par))
    qi = iota((QN, 128), 0)
    q_tile = 8 * ((qi % KB) // ROWS) + 2 * (qi // KB) + x // 2
    expand[...] = one_hot(iota((QN, 128), 1) == q_tile)
    stat[...] = jnp.where(iota((8, QN), 0) == 0, -3e38, 0.0)
    out_t[...] = jnp.zeros_like(out_t)
    dqt[...] = jnp.zeros_like(dqt)
    tsum[...] = jnp.zeros_like(tsum)
    square[...] = jnp.zeros((128, 128), F32)

    await_bytes(mz.at[pl.ds(0, 7)], recv.at[G_MZ])
    total = mz[0]
    for i in range(1, NZ):
        total = total + mz[i]
    mx[n_plane] = total
    to_plane(mx, G_MX)

    await_bytes(stk.at[pl.ds(0, 7)], recv.at[G_AK])

    @each(NXC, core)
    def _(d):
        p = ((x + d // 2) % NX) * 2 + d % 2
        put(kvb.at[xc], kvb.at[xc], G_KV, dev(z, y, p, zh), slot=S_KV + xc)

    await_bytes(stq.at[pl.ds(0, 7)], recv.at[G_AQ])

    @each(NY, y)
    def _(p):
        put(qd.at[y], qd.at[y], G_QD, dev(z, p, xc, zh))

    await_bytes(mx.at[pl.ds(0, PLANE - 1)], recv.at[G_MX])
    codes = jnp.concatenate([mx[i] for i in range(PLANE)], axis=0).astype(BF16)
    pick_b, pick_a = iota((256, 128), 0) // 64, iota((256, 128), 0) % 64
    picked = dot_nt(one_hot(iota((256, 128), 1) == (pick_a // 8) * 16 + (pick_a % 4) * 4 + pick_b), codes)
    same_half = (iota((256, 32), 0) // 4) % 2 == iota((256, 32), 1) // 16
    picked = jnp.where(same_half, picked, 0.0).astype(BF16)
    fcode = jnp.zeros((64, 128), F32)
    for b in range(4):
        spread = one_hot(iota((32, 128), 1) == 4 * (iota((32, 128), 0) % 16) + b)
        fcode = fcode + dot_nn(picked[b * 64 : (b + 1) * 64], spread)
    square[0:64] = fcode
    gcode = jnp.transpose(square[...])[0:64]
    own_proj = projt_ref[pl.ds(zf, 1), :]
    type_bias = jnp.sum(table_ref[...] * own_proj, axis=1, keepdims=True)
    type_bias = jnp.broadcast_to(type_bias, (TYPES, 128))
    bias = jnp.zeros((64, 128), F32)
    for t in range(TYPES):
        here = type_bias[t : t + 1, :]
        bias = bias + jnp.where(fcode == t + 1.0, here, 0.0) + jnp.where(gcode == t + 1.0, here, 0.0)
    bias = jnp.where(fcode + gcode > 0.0, bias, MASKED)
    sel_n = iota((128, 128), 1)
    sel_b = sel_n % 16
    column = iota((128, 128), 0) == 8 * (sel_b // 2) + 2 * y + sel_b % 2
    columns = jnp.zeros((64, 128), F32)
    for part, piece in enumerate(split3(bias)):
        columns = columns + dot_nn(piece, one_hot(column & (sel_n // 16 == part)))
    columns = columns.astype(BF16)
    qt[128:256, :] = jnp.transpose(dot_nn(expand[:, 0:64], columns)).astype(BF16)
    kr = iota((16, 64), 0)
    pick_rows = one_hot(iota((16, 64), 1) == 8 * (kr % 8) + 2 * y + kr // 8)
    fsel[...] = dot_nn(pick_rows, gcode.astype(BF16))
    gsel[...] = dot_nn(pick_rows, fcode.astype(BF16))

    await_bytes(qd.at[pl.ds(0, 3)], recv.at[G_QD])
    low_lanes = jnp.where(lanes < HD, 1.0, 0.0)
    both = qd[...].reshape(QN, 128).astype(F32)
    q_only = both * low_lanes
    d_only = both * (1.0 - low_lanes)
    q0[...] = q_only.astype(BF16)
    d0[...] = d_only.astype(BF16)
    qt[0:128, :] = jnp.transpose(q_only).astype(BF16)
    dt[...] = jnp.transpose(d_only).astype(BF16)

    def block_at(i, c):
        return ((x + i) % NX) * 2 + (core + c) % 2

    order = [block_at(i, c) for i in reversed(FAR_FIRST) for c in range(NC)]

    def products(s):
        j = order[s]
        if s > 0:
            await_bytes(kvb.at[j], recv.at[S_KV + j])
        kv = kvb[j]
        sbuf[s % 2] = dot_nn(jnp.concatenate([kv, konehot[j // 4]], axis=1), qt[...])
        dbuf[s % 2] = dot_nn(kv, dt[...])

    def forward(s):
        j = order[s]
        kvt = jnp.transpose(kvb[j])
        for cs in CHUNKS:
            scores = sbuf[s % 2, :, cs]
            dp = dbuf[s % 2, :, cs]
            dprob[j, :, cs] = dp
            old = stat[0:1, cs]
            top = jnp.maximum(old, jnp.max(scores, axis=0, keepdims=True))
            e = jnp.exp(scores - top)
            shrink = jnp.exp(old - top)
            eb = e.astype(BF16)
            exps[j, :, cs] = eb
            stat[0:1, cs] = top
            stat[1:2, cs] = stat[1:2, cs] * shrink + jnp.sum(e, axis=0, keepdims=True)
            stat[2:3, cs] = stat[2:3, cs] * shrink + jnp.sum(e * dp, axis=0, keepdims=True)
            tops[j, 0:1, cs] = top
            out_t[:, cs] = out_t[:, cs] * shrink + dot_nn(kvt, eb)

    products(0)
    for s in range(NXC):
        if s + 1 < NXC:
            products(s + 1)
        forward(s)

    for i in range(3):
        packed[y, i] = fold(stat[i : i + 1, :])

    @each(NY, y)
    def _(p):
        put(packed.at[y], packed.at[y], G_ST, dev(z, p, xc, zh))

    await_bytes(packed.at[pl.ds(0, 3)], recv.at[G_ST])
    top = packed[0, 0]
    for i in range(1, NY):
        top = jnp.maximum(top, packed[i, 0])
    weight_sum = jnp.zeros((8, 128), F32)
    delta = jnp.zeros((8, 128), F32)
    for i in range(NY):
        scale = jnp.exp(packed[i, 0] - top)
        weight_sum = weight_sum + packed[i, 1] * scale
        delta = delta + packed[i, 2] * scale
    delta = unfold(delta / weight_sum)
    logsum = unfold(top + jnp.log(weight_sum))
    own_scale = unfold(jnp.exp(packed[y, 0] - top) / weight_sum)
    for p in range(NY):
        cs = slice(p * KB, (p + 1) * KB)
        osend[p] = (out_t[HD : 2 * HD, cs] * own_scale[:, cs]).astype(BF16)
    orecv[y] = osend[y]

    def backward(j):
        kv = kvb[j]
        kvt = jnp.transpose(kv)
        dkv = jnp.zeros((KB, 128), F32)
        for cs in CHUNKS:
            sigma = jnp.exp(tops[j, 0:1, cs] - logsum[:, cs])
            p = exps[j, :, cs].astype(F32) * sigma
            ds = p * (dprob[j, :, cs] - delta[:, cs])
            pb = p.astype(BF16)
            dsb = ds.astype(BF16)
            dkv = dkv + dot_nn(pb, d0[cs]) + dot_nn(dsb, q0[cs])
            dqt[:, cs] = dqt[:, cs] + dot_nn(kvt, dsb)
            tsum[j // 4, :, cs] = tsum[j // 4, :, cs] + jnp.sum(ds.reshape(NZ, ROWS, QCHUNK), axis=1)
        return dkv

    other = (core + 1) % 2

    def add_partner(n, dkv):
        await_bytes(precv.at[n], recv.at[S_PR + n])
        return dkv + precv[n].astype(F32)

    def pass_on(n, dkv):
        rsend[n] = add_partner(n, dkv).astype(BF16)
        put(rsend.at[n], rrecv.at[x], G_RS, dev(z, y, block_at(FAR_FIRST[n], 0), zh))

    partials = []
    for n, i in enumerate(FAR_FIRST):
        psend[n] = backward(block_at(i, 1)).astype(BF16)
        put(psend.at[n], precv.at[n], G_PR, dev(z, y, x * 2 + other, zh), slot=S_PR + n)
        if n == 0:

            @each(NY, y)
            def _(p):
                put(osend.at[p], orecv.at[y], G_O, dev(z, p, xc, zh))

        partials.append(backward(block_at(i, 0)))
        if n == 2:
            pass_on(0, partials[0])
    pass_on(1, partials[1])
    pass_on(2, partials[2])

    for p in range(NY):
        dsend[p] = (dqt[0:HD, p * KB : (p + 1) * KB] * 0.125).astype(BF16)
    drecv[y] = dsend[y]

    @each(NY, y)
    def _(p):
        put(dsend.at[p], drecv.at[y], G_DQ, dev(z, p, xc, zh))

    sums = jnp.zeros((16, 128), F32)
    for piece in split3(tsum[...].reshape(16, QN)):
        sums = sums + dot_nn(piece, expand[...])
    for t in range(TYPES):
        hits = jnp.where(fsel[...] == t + 1.0, sums, 0.0) + jnp.where(gsel[...] == t + 1.0, sums, 0.0)
        square[t : t + 1, :] = jnp.sum(hits, axis=0, keepdims=True)
    square[TYPES:64, :] = jnp.zeros((64 - TYPES, 128), F32)
    tx[n_plane] = jnp.sum(jnp.transpose(square[...]), axis=0, keepdims=True)
    to_plane(tx, G_TX)

    await_bytes(orecv.at[pl.ds(0, 3)], recv.at[G_O])
    att = orecv[0].astype(F32)
    for p in range(1, NY):
        att = att + orecv[p].astype(F32)
    x0s[...] = half_rows(jnp.transpose(att))

    @each(NZ, z)
    def _(p):
        put(x0s.at[p], x0r.at[z], G_X0, dev(p, y, xc, zh))

    x0r[z] = x0s[z]

    own = add_partner(NX - 1, partials[3])
    await_bytes(rrecv.at[pl.ds(0, 3)], recv.at[G_RS])
    for i in (1, 2, 3):
        own = own + rrecv[(x + i) % NX].astype(F32)
    x2s[...] = own.astype(BF16).reshape(NZ, ROWS, 128)

    @each(NZ, z)
    def _(p):
        put(x2s.at[p], x2r.at[z], G_X2, dev(p, y, xc, zh))

    x2r[z] = x2s[z]

    await_bytes(drecv.at[pl.ds(0, 3)], recv.at[G_DQ])
    dq = drecv[0].astype(F32) + drecv[1].astype(F32) + drecv[2].astype(F32) + drecv[3].astype(F32)
    x1s[...] = half_rows(jnp.transpose(dq))

    @each(NZ, z)
    def _(p):
        put(x1s.at[p], x1r.at[z], G_X1, dev(p, y, xc, zh))

    x1r[z] = x1s[z]

    await_bytes(tx.at[pl.ds(0, PLANE - 1)], recv.at[G_TX])
    total = tx[0]
    for i in range(1, PLANE):
        total = total + tx[i]
    tz[zf] = total

    @each(2 * NZ, zf)
    def _(p):
        put(tz.at[zf], tz.at[zf], G_TZ, dev(p % NZ, y, xc, p // NZ))

    for ref, group in (
        (stk.at[pl.ds(0, 7)], G_AK), (stq.at[pl.ds(0, 7)], G_AQ), (mz.at[pl.ds(0, 7)], G_MZ),
        (mx.at[pl.ds(0, PLANE - 1)], G_MX), (qd.at[pl.ds(0, 3)], G_QD),
        (kvb.at[pl.ds(0, 7)], G_KV), (packed.at[pl.ds(0, 3)], G_ST), (osend.at[pl.ds(0, 3)], G_O),
        (psend.at[pl.ds(0, 4)], G_PR), (dsend.at[pl.ds(0, 3)], G_DQ), (rsend.at[pl.ds(0, 3)], G_RS),
        (tx.at[pl.ds(0, PLANE - 1)], G_TX), (x0s.at[pl.ds(0, 7)], G_X0),
        (x2s.at[pl.ds(0, 7)], G_X2), (x1s.at[pl.ds(0, 7)], G_X1), (tz.at[pl.ds(0, 15)], G_TZ),
    ):
        await_bytes(ref, send.at[group])

    await_bytes(x0r.at[pl.ds(0, 7)], recv.at[G_X0])
    x0_ref[...] = x0r[...]
    await_bytes(x2r.at[pl.ds(0, 7)], recv.at[G_X2])
    x2_ref[...] = x2r[...]
    await_bytes(x1r.at[pl.ds(0, 7)], recv.at[G_X1])
    x1_ref[...] = x1r[...]
    await_bytes(tz.at[pl.ds(0, 15)], recv.at[G_TZ])
    tg_ref[...] = jnp.concatenate([tz[h] for h in range(2 * NZ)], axis=0)


def lay_out(
    x0_ref, x1_ref, x2_ref, tg_ref, table_ref, projt_ref,
    att_ref, dq_ref, dk_ref, dv_ref, dtable_ref, dprojt_ref, square,
):
    low, high = slice(0, HD), slice(HD, 2 * HD)
    for h in range(NZ):
        cols = slice(h * HD, (h + 1) * HD)
        att_ref[0:HALF, cols] = x0_ref[h][:, low]
        att_ref[HALF:ROWS, cols] = x0_ref[h][:, high]
        dq_ref[0:HALF, cols] = x1_ref[h][:, low].astype(F32)
        dq_ref[HALF:ROWS, cols] = x1_ref[h][:, high].astype(F32)
        dk_ref[:, cols] = x2_ref[h][:, low].astype(F32)
        dv_ref[:, cols] = x2_ref[h][:, high].astype(F32)
    tg = tg_ref[...]
    square[...] = jnp.zeros((128, 128), F32)
    square[0:16] = tg
    tg_t = jnp.transpose(square[...])
    dtable = jnp.zeros((TYPES, 128), F32)
    dprojt = jnp.zeros((2 * NZ, 128), F32)
    for i in range(16):
        dtable = dtable + tg_t[0:16, i : i + 1] * projt_ref[i : i + 1, :]
        dprojt = dprojt + tg[:, i : i + 1] * table_ref[i : i + 1, :]
    dtable_ref[...] = dtable
    dprojt_ref[...] = dprojt


def per_device(node_query, node_key, node_value, out_grad, tile_mask, tile_type, edge_table, edge_proj):
    vmem = pl.BlockSpec(memory_space=pltpu.VMEM)
    smem = pl.BlockSpec(memory_space=pltpu.SMEM)
    half = (ROWS, NZ * HD)
    proj_t = edge_proj.T
    spread = pl.pallas_call(
        kernel,
        out_shape=(
            jax.ShapeDtypeStruct((NZ, HALF, 128), BF16),
            jax.ShapeDtypeStruct((NZ, HALF, 128), BF16),
            jax.ShapeDtypeStruct((NZ, ROWS, 128), BF16),
            jax.ShapeDtypeStruct((2 * NZ, 128), F32),
        ),
        in_specs=[vmem] * 4 + [smem] * 2 + [vmem] * 2,
        out_specs=(vmem,) * 4,
        scratch_shapes=[
            pltpu.VMEM((NZ, ROWS, 128), BF16),
            pltpu.VMEM((NZ, ROWS, 128), BF16),
            pltpu.VMEM((NY, KB, 128), BF16),
            pltpu.VMEM((NXC, KB, 128), BF16),
            pltpu.VMEM((QN, 128), BF16),
            pltpu.VMEM((QN, 128), BF16),
            pltpu.VMEM((256, QN), BF16),
            pltpu.VMEM((128, QN), BF16),
            pltpu.VMEM((2, KB, 128), BF16),
            pltpu.VMEM((QN, 128), BF16),
            pltpu.VMEM((NZ, 1, 128), F32),
            pltpu.VMEM((PLANE, 1, 128), F32),
            pltpu.VMEM((16, 128), F32),
            pltpu.VMEM((16, 128), F32),
            pltpu.VMEM((128, 128), F32),
            pltpu.VMEM((2, KB, QN), F32),
            pltpu.VMEM((2, KB, QN), F32),
            pltpu.VMEM((NXC, KB, QN), BF16),
            pltpu.VMEM((NXC, KB, QN), F32),
            pltpu.VMEM((NXC, 8, QN), F32),
            pltpu.VMEM((8, QN), F32),
            pltpu.VMEM((NY, 3, 8, 128), F32),
            pltpu.VMEM((128, QN), F32),
            pltpu.VMEM((128, QN), F32),
            pltpu.VMEM((2, NZ, QN), F32),
            pltpu.VMEM((NY, HD, KB), BF16),
            pltpu.VMEM((NY, HD, KB), BF16),
            pltpu.VMEM((NY, HD, KB), BF16),
            pltpu.VMEM((NY, HD, KB), BF16),
            pltpu.VMEM((NX, KB, 128), BF16),
            pltpu.VMEM((NX, KB, 128), BF16),
            pltpu.VMEM((NX, KB, 128), BF16),
            pltpu.VMEM((NX, KB, 128), BF16),
            pltpu.VMEM((PLANE, 1, 128), F32),
            pltpu.VMEM((2 * NZ, 1, 128), F32),
            pltpu.VMEM((NZ, HALF, 128), BF16),
            pltpu.VMEM((NZ, HALF, 128), BF16),
            pltpu.VMEM((NZ, HALF, 128), BF16),
            pltpu.VMEM((NZ, HALF, 128), BF16),
            pltpu.VMEM((NZ, ROWS, 128), BF16),
            pltpu.VMEM((NZ, ROWS, 128), BF16),
            pltpu.SemaphoreType.DMA((16,)),
            pltpu.SemaphoreType.DMA((N_SEMS,)),
        ],
        compiler_params=pltpu.CompilerParams(
            collective_id=0, has_side_effects=True, vmem_limit_bytes=56 * 1024 * 1024
        ),
        cost_estimate=pl.CostEstimate(
            flops=12 * QN * NXC * KB * 128, bytes_accessed=600_000, transcendentals=QN * NXC * KB
        ),
    )(node_query, node_key, node_value, out_grad, tile_mask, tile_type, edge_table, proj_t)
    att, dq, dk, dv, dtable, dprojt = pl.pallas_call(
        lay_out,
        out_shape=(
            jax.ShapeDtypeStruct(half, BF16),
            jax.ShapeDtypeStruct(half, F32),
            jax.ShapeDtypeStruct(half, F32),
            jax.ShapeDtypeStruct(half, F32),
            jax.ShapeDtypeStruct((TYPES, 128), F32),
            jax.ShapeDtypeStruct((2 * NZ, 128), F32),
        ),
        in_specs=[vmem] * 6,
        out_specs=(vmem,) * 6,
        scratch_shapes=[pltpu.VMEM((128, 128), F32)],
    )(*spread, edge_table, proj_t)
    return att, dq, dk, dv, dtable, dprojt.T


def solution(mesh):
    split = P("grid", "head")
    return jax.shard_map(
        per_device,
        mesh=mesh,
        in_specs=(split, split, split, split, P("grid", None, None), P("grid", None, None), P(), P()),
        out_specs=(split, split, split, split, P(), P()),
        check_vma=False,
    )
```

```python
import jax
import jax.numpy as jnp
from jax import lax
from jax.experimental import pallas as pl
from jax.experimental.pallas import tpu as pltpu
from jax.sharding import PartitionSpec as P

F32 = jnp.float32
BF16 = jnp.bfloat16
MESH = pl.DeviceIdType.MESH

NZ, NY, NX, NC = 8, 4, 4, 2
NXC = NX * NC
PLANE = NY * NXC
ROWS = 32
HALF = ROWS // 2
HD = 64
TYPES = 16
QN = NY * NZ * ROWS
KB = NZ * ROWS
MASKED = -1e30
QCHUNK = 256
CHUNKS = [slice(c * QCHUNK, (c + 1) * QCHUNK) for c in range(QN // QCHUNK)]
FAR_FIRST = (2, 3, 1, 0)

(G_AQ, G_AK, G_MZ, G_MX, G_QD, G_ST, G_O, G_DQ, G_RS, G_TX, G_TZ, G_X0, G_X1, G_X2, G_KV, G_PR) = range(16)
S_KV = 16
S_PR = S_KV + NXC
N_SEMS = S_PR + NX


def dot_nt(a, b):
    return lax.dot_general(a, b, (((1,), (1,)), ((), ())), preferred_element_type=F32)


def dot_nn(a, b):
    return lax.dot_general(a, b, (((1,), (0,)), ((), ())), preferred_element_type=F32)


def split3(x):
    hi = x.astype(BF16)
    rest = x - hi.astype(F32)
    mid = rest.astype(BF16)
    low = (rest - mid.astype(F32)).astype(BF16)
    return hi, mid, low


def iota(shape, dim):
    return lax.broadcasted_iota(jnp.int32, shape, dim)


def one_hot(condition):
    return jnp.where(condition, 1.0, 0.0).astype(BF16)


def fold(row):
    return jnp.concatenate([row[:, i * 128 : (i + 1) * 128] for i in range(QN // 128)], axis=0)


def unfold(square):
    return jnp.concatenate([square[i : i + 1, :] for i in range(QN // 128)], axis=1)


def half_rows(full):
    full = full.reshape(NZ, ROWS, HD)
    return jnp.concatenate([full[:, 0:HALF], full[:, HALF:ROWS]], axis=2).astype(BF16)


def kernel(
    q_ref, k_ref, v_ref, do_ref, mask_ref, type_ref, table_ref, projt_ref,
    x0_ref, x1_ref, x2_ref, tg_ref,
    stq, stk, qd, kvb, q0, d0, qt, dt, konehot, expand,
    mz, mx, fsel, gsel, square,
    sbuf, dbuf, exps, dprob, tops, stat, packed, out_t, dqt, tsum,
    osend, orecv, dsend, drecv, psend, precv, rsend, rrecv,
    tx, tz, x0s, x0r, x1s, x1r, x2s, x2r,
    send, recv,
):
    g = lax.axis_index("grid")
    zh = lax.axis_index("head")
    core = g % 2
    x = (g // 2) % 4
    y = (g // 8) % 4
    z = g // 32
    xc = g % 8
    n_plane = g % PLANE
    zf = zh * NZ + z

    def dev(z_, y_, xc_, zh_):
        return ((z_ * NY + y_) * NXC + xc_, zh_)

    def put(src, dst, group, where, slot=None):
        pltpu.make_async_remote_copy(
            src_ref=src, dst_ref=dst, send_sem=send.at[group],
            recv_sem=recv.at[group if slot is None else slot],
            device_id=where, device_id_type=MESH,
        ).start()

    def await_bytes(ref, sem):
        pltpu.make_async_copy(ref, ref, sem).wait()

    def in_plane(d):
        return (z * PLANE + (n_plane + d) % PLANE, zh)

    def to_plane(slots, group):
        def step(d, carry):
            put(slots.at[n_plane], slots.at[n_plane], group, in_plane(d))
            return carry

        lax.fori_loop(1, PLANE, step, 0)

    def each(count, me):
        def run(act):
            def step(d, carry):
                act((me + d) % count)
                return carry

            lax.fori_loop(1, count, step, 0)

        return run

    barrier = pltpu.get_barrier_semaphore()

    @each(2 * NZ, zf)
    def _(p):
        pl.semaphore_signal(barrier, inc=1, device_id=dev(p % NZ, y, xc, p // NZ), device_id_type=MESH)

    def greet(d, carry):
        pl.semaphore_signal(barrier, inc=1, device_id=in_plane(d), device_id_type=MESH)
        return carry

    lax.fori_loop(1, PLANE, greet, 0)

    lanes = iota((1, 128), 1)
    code = jnp.zeros((1, 128), jnp.int32)
    for a in range(4):
        for b in range(4):
            value = mask_ref[0, a, b] * (type_ref[0, a, b] + 1)
            code = jnp.where(lanes == z * 16 + (a * 4 + b), value, code)
    mz[z] = code.astype(F32)

    for h in range(NZ):
        cols = slice(h * HD, (h + 1) * HD)
        scaled = (q_ref[:, cols].astype(F32) * 0.125).astype(BF16)
        stq[h] = jnp.concatenate([scaled, do_ref[:, cols]], axis=1)
        stk[h] = jnp.concatenate([k_ref[:, cols], v_ref[:, cols]], axis=1)

    pl.semaphore_wait(barrier, PLANE - 1 + 2 * NZ - 1)

    own_rows = pl.ds(pl.multiple_of(z * ROWS, ROWS), ROWS)

    @each(NZ, z)
    def _(p):
        put(mz.at[z], mz.at[z], G_MZ, dev(p, y, xc, zh))

    @each(NZ, z)
    def _(p):
        put(stk.at[p], kvb.at[xc, own_rows], G_AK, dev(p, y, xc, zh))
        put(stq.at[p], qd.at[y, own_rows], G_AQ, dev(p, y, xc, zh))

    kvb[xc, own_rows] = stk[z]
    qd[y, own_rows] = stq[z]

    kn = iota((KB, 128), 1)
    kt = iota((KB, 128), 0) // ROWS
    for par in range(2):
        konehot[par] = one_hot((kn < 48) & (kn % 16 == 2 * kt + par))
    qi = iota((QN, 128), 0)
    q_tile = 8 * ((qi % KB) // ROWS) + 2 * (qi // KB) + x // 2
    expand[...] = one_hot(iota((QN, 128), 1) == q_tile)
    stat[...] = jnp.where(iota((8, QN), 0) == 0, -3e38, 0.0)
    out_t[...] = jnp.zeros_like(out_t)
    dqt[...] = jnp.zeros_like(dqt)
    tsum[...] = jnp.zeros_like(tsum)
    square[...] = jnp.zeros((128, 128), F32)

    await_bytes(mz.at[pl.ds(0, 7)], recv.at[G_MZ])
    total = mz[0]
    for i in range(1, NZ):
        total = total + mz[i]
    mx[n_plane] = total
    to_plane(mx, G_MX)

    await_bytes(stk.at[pl.ds(0, 7)], recv.at[G_AK])

    @each(NXC, core)
    def _(d):
        p = ((x + d // 2) % NX) * 2 + d % 2
        put(kvb.at[xc], kvb.at[xc], G_KV, dev(z, y, p, zh), slot=S_KV + xc)

    await_bytes(stq.at[pl.ds(0, 7)], recv.at[G_AQ])

    @each(NY, y)
    def _(p):
        put(qd.at[y], qd.at[y], G_QD, dev(z, p, xc, zh))

    await_bytes(mx.at[pl.ds(0, PLANE - 1)], recv.at[G_MX])
    codes = jnp.concatenate([mx[i] for i in range(PLANE)], axis=0).astype(BF16)
    pick_b, pick_a = iota((256, 128), 0) // 64, iota((256, 128), 0) % 64
    picked = dot_nt(one_hot(iota((256, 128), 1) == (pick_a // 8) * 16 + (pick_a % 4) * 4 + pick_b), codes)
    same_half = (iota((256, 32), 0) // 4) % 2 == iota((256, 32), 1) // 16
    picked = jnp.where(same_half, picked, 0.0).astype(BF16)
    fcode = jnp.zeros((64, 128), F32)
    for b in range(4):
        spread = one_hot(iota((32, 128), 1) == 4 * (iota((32, 128), 0) % 16) + b)
        fcode = fcode + dot_nn(picked[b * 64 : (b + 1) * 64], spread)
    square[0:64] = fcode
    gcode = jnp.transpose(square[...])[0:64]
    own_proj = projt_ref[pl.ds(zf, 1), :]
    type_bias = jnp.sum(table_ref[...] * own_proj, axis=1, keepdims=True)
    type_bias = jnp.broadcast_to(type_bias, (TYPES, 128))
    bias = jnp.zeros((64, 128), F32)
    for t in range(TYPES):
        here = type_bias[t : t + 1, :]
        bias = bias + jnp.where(fcode == t + 1.0, here, 0.0) + jnp.where(gcode == t + 1.0, here, 0.0)
    bias = jnp.where(fcode + gcode > 0.0, bias, MASKED)
    sel_n = iota((128, 128), 1)
    sel_b = sel_n % 16
    column = iota((128, 128), 0) == 8 * (sel_b // 2) + 2 * y + sel_b % 2
    columns = jnp.zeros((64, 128), F32)
    for part, piece in enumerate(split3(bias)):
        columns = columns + dot_nn(piece, one_hot(column & (sel_n // 16 == part)))
    columns = columns.astype(BF16)
    qt[128:256, :] = jnp.transpose(dot_nn(expand[:, 0:64], columns)).astype(BF16)
    kr = iota((16, 64), 0)
    pick_rows = one_hot(iota((16, 64), 1) == 8 * (kr % 8) + 2 * y + kr // 8)
    fsel[...] = dot_nn(pick_rows, gcode.astype(BF16))
    gsel[...] = dot_nn(pick_rows, fcode.astype(BF16))

    await_bytes(qd.at[pl.ds(0, 3)], recv.at[G_QD])
    low_lanes = jnp.where(lanes < HD, 1.0, 0.0)
    both = qd[...].reshape(QN, 128).astype(F32)
    q_only = both * low_lanes
    d_only = both * (1.0 - low_lanes)
    q0[...] = q_only.astype(BF16)
    d0[...] = d_only.astype(BF16)
    qt[0:128, :] = jnp.transpose(q_only).astype(BF16)
    dt[...] = jnp.transpose(d_only).astype(BF16)

    def block_at(i, c):
        return ((x + i) % NX) * 2 + (core + c) % 2

    order = [block_at(i, c) for i in reversed(FAR_FIRST) for c in range(NC)]

    def products(s):
        j = order[s]
        if s > 0:
            await_bytes(kvb.at[j], recv.at[S_KV + j])
        kv = kvb[j]
        sbuf[s % 2] = dot_nn(jnp.concatenate([kv, konehot[j // 4]], axis=1), qt[...])
        dbuf[s % 2] = dot_nn(kv, dt[...])

    def forward(s):
        j = order[s]
        kvt = jnp.transpose(kvb[j])
        for cs in CHUNKS:
            scores = sbuf[s % 2, :, cs]
            dp = dbuf[s % 2, :, cs]
            dprob[j, :, cs] = dp
            old = stat[0:1, cs]
            top = jnp.maximum(old, jnp.max(scores, axis=0, keepdims=True))
            e = jnp.exp(scores - top)
            shrink = jnp.exp(old - top)
            eb = e.astype(BF16)
            exps[j, :, cs] = eb
            stat[0:1, cs] = top
            stat[1:2, cs] = stat[1:2, cs] * shrink + jnp.sum(e, axis=0, keepdims=True)
            stat[2:3, cs] = stat[2:3, cs] * shrink + jnp.sum(e * dp, axis=0, keepdims=True)
            tops[j, 0:1, cs] = top
            out_t[:, cs] = out_t[:, cs] * shrink + dot_nn(kvt, eb)

    products(0)
    for s in range(NXC):
        if s + 1 < NXC:
            products(s + 1)
        forward(s)

    for i in range(3):
        packed[y, i] = fold(stat[i : i + 1, :])

    @each(NY, y)
    def _(p):
        put(packed.at[y], packed.at[y], G_ST, dev(z, p, xc, zh))

    await_bytes(packed.at[pl.ds(0, 3)], recv.at[G_ST])
    top = packed[0, 0]
    for i in range(1, NY):
        top = jnp.maximum(top, packed[i, 0])
    weight_sum = jnp.zeros((8, 128), F32)
    delta = jnp.zeros((8, 128), F32)
    for i in range(NY):
        scale = jnp.exp(packed[i, 0] - top)
        weight_sum = weight_sum + packed[i, 1] * scale
        delta = delta + packed[i, 2] * scale
    delta = unfold(delta / weight_sum)
    logsum = unfold(top + jnp.log(weight_sum))
    own_scale = unfold(jnp.exp(packed[y, 0] - top) / weight_sum)
    for p in range(NY):
        cs = slice(p * KB, (p + 1) * KB)
        osend[p] = (out_t[HD : 2 * HD, cs] * own_scale[:, cs]).astype(BF16)
    orecv[y] = osend[y]

    def backward(j):
        kv = kvb[j]
        kvt = jnp.transpose(kv)
        dkv = jnp.zeros((KB, 128), F32)
        for cs in CHUNKS:
            sigma = jnp.exp(tops[j, 0:1, cs] - logsum[:, cs])
            p = exps[j, :, cs].astype(F32) * sigma
            ds = p * (dprob[j, :, cs] - delta[:, cs])
            pb = p.astype(BF16)
            dsb = ds.astype(BF16)
            dkv = dkv + dot_nn(pb, d0[cs]) + dot_nn(dsb, q0[cs])
            dqt[:, cs] = dqt[:, cs] + dot_nn(kvt, dsb)
            tsum[j // 4, :, cs] = tsum[j // 4, :, cs] + jnp.sum(ds.reshape(NZ, ROWS, QCHUNK), axis=1)
        return dkv

    other = (core + 1) % 2

    def add_partner(n, dkv):
        await_bytes(precv.at[n], recv.at[S_PR + n])
        return dkv + precv[n].astype(F32)

    def pass_on(n, dkv):
        rsend[n] = add_partner(n, dkv).astype(BF16)
        put(rsend.at[n], rrecv.at[x], G_RS, dev(z, y, block_at(FAR_FIRST[n], 0), zh))

    partials = []
    for n, i in enumerate(FAR_FIRST):
        psend[n] = backward(block_at(i, 1)).astype(BF16)
        put(psend.at[n], precv.at[n], G_PR, dev(z, y, x * 2 + other, zh), slot=S_PR + n)
        if n == 0:

            @each(NY, y)
            def _(p):
                put(osend.at[p], orecv.at[y], G_O, dev(z, p, xc, zh))

        partials.append(backward(block_at(i, 0)))
        if n == 2:
            pass_on(0, partials[0])
    pass_on(1, partials[1])
    pass_on(2, partials[2])

    sums = jnp.zeros((16, 128), F32)
    for piece in split3(tsum[...].reshape(16, QN)):
        sums = sums + dot_nn(piece, expand[...])
    for t in range(TYPES):
        hits = jnp.where(fsel[...] == t + 1.0, sums, 0.0) + jnp.where(gsel[...] == t + 1.0, sums, 0.0)
        square[t : t + 1, :] = jnp.sum(hits, axis=0, keepdims=True)
    square[TYPES:64, :] = jnp.zeros((64 - TYPES, 128), F32)
    tx[n_plane] = jnp.sum(jnp.transpose(square[...]), axis=0, keepdims=True)
    to_plane(tx, G_TX)

    for p in range(NY):
        dsend[p] = (dqt[0:HD, p * KB : (p + 1) * KB] * 0.125).astype(BF16)
    drecv[y] = dsend[y]

    @each(NY, y)
    def _(p):
        put(dsend.at[p], drecv.at[y], G_DQ, dev(z, p, xc, zh))

    await_bytes(orecv.at[pl.ds(0, 3)], recv.at[G_O])
    att = orecv[0].astype(F32)
    for p in range(1, NY):
        att = att + orecv[p].astype(F32)
    x0s[...] = half_rows(jnp.transpose(att))

    @each(NZ, z)
    def _(p):
        put(x0s.at[p], x0r.at[z], G_X0, dev(p, y, xc, zh))

    x0r[z] = x0s[z]

    own = add_partner(NX - 1, partials[3])
    await_bytes(rrecv.at[pl.ds(0, 3)], recv.at[G_RS])
    for i in (1, 2, 3):
        own = own + rrecv[(x + i) % NX].astype(F32)
    x2s[...] = own.astype(BF16).reshape(NZ, ROWS, 128)

    @each(NZ, z)
    def _(p):
        put(x2s.at[p], x2r.at[z], G_X2, dev(p, y, xc, zh))

    x2r[z] = x2s[z]

    await_bytes(drecv.at[pl.ds(0, 3)], recv.at[G_DQ])
    dq = drecv[0].astype(F32) + drecv[1].astype(F32) + drecv[2].astype(F32) + drecv[3].astype(F32)
    x1s[...] = half_rows(jnp.transpose(dq))

    @each(NZ, z)
    def _(p):
        put(x1s.at[p], x1r.at[z], G_X1, dev(p, y, xc, zh))

    x1r[z] = x1s[z]

    await_bytes(tx.at[pl.ds(0, PLANE - 1)], recv.at[G_TX])
    total = tx[0]
    for i in range(1, PLANE):
        total = total + tx[i]
    tz[zf] = total

    @each(2 * NZ, zf)
    def _(p):
        put(tz.at[zf], tz.at[zf], G_TZ, dev(p % NZ, y, xc, p // NZ))

    for ref, group in (
        (stk.at[pl.ds(0, 7)], G_AK), (stq.at[pl.ds(0, 7)], G_AQ), (mz.at[pl.ds(0, 7)], G_MZ),
        (mx.at[pl.ds(0, PLANE - 1)], G_MX), (qd.at[pl.ds(0, 3)], G_QD),
        (kvb.at[pl.ds(0, 7)], G_KV), (packed.at[pl.ds(0, 3)], G_ST), (osend.at[pl.ds(0, 3)], G_O),
        (psend.at[pl.ds(0, 4)], G_PR), (dsend.at[pl.ds(0, 3)], G_DQ), (rsend.at[pl.ds(0, 3)], G_RS),
        (tx.at[pl.ds(0, PLANE - 1)], G_TX), (x0s.at[pl.ds(0, 7)], G_X0),
        (x2s.at[pl.ds(0, 7)], G_X2), (x1s.at[pl.ds(0, 7)], G_X1), (tz.at[pl.ds(0, 15)], G_TZ),
    ):
        await_bytes(ref, send.at[group])

    await_bytes(x0r.at[pl.ds(0, 7)], recv.at[G_X0])
    x0_ref[...] = x0r[...]
    await_bytes(x2r.at[pl.ds(0, 7)], recv.at[G_X2])
    x2_ref[...] = x2r[...]
    await_bytes(x1r.at[pl.ds(0, 7)], recv.at[G_X1])
    x1_ref[...] = x1r[...]
    await_bytes(tz.at[pl.ds(0, 15)], recv.at[G_TZ])
    tg_ref[...] = jnp.concatenate([tz[h] for h in range(2 * NZ)], axis=0)


def lay_out(
    x0_ref, x1_ref, x2_ref, tg_ref, table_ref, projt_ref,
    att_ref, dq_ref, dk_ref, dv_ref, dtable_ref, dprojt_ref, square,
):
    low, high = slice(0, HD), slice(HD, 2 * HD)
    for h in range(NZ):
        cols = slice(h * HD, (h + 1) * HD)
        att_ref[0:HALF, cols] = x0_ref[h][:, low]
        att_ref[HALF:ROWS, cols] = x0_ref[h][:, high]
        dq_ref[0:HALF, cols] = x1_ref[h][:, low].astype(F32)
        dq_ref[HALF:ROWS, cols] = x1_ref[h][:, high].astype(F32)
        dk_ref[:, cols] = x2_ref[h][:, low].astype(F32)
        dv_ref[:, cols] = x2_ref[h][:, high].astype(F32)
    tg = tg_ref[...]
    square[...] = jnp.zeros((128, 128), F32)
    square[0:16] = tg
    tg_t = jnp.transpose(square[...])
    dtable = jnp.zeros((TYPES, 128), F32)
    dprojt = jnp.zeros((2 * NZ, 128), F32)
    for i in range(16):
        dtable = dtable + tg_t[0:16, i : i + 1] * projt_ref[i : i + 1, :]
        dprojt = dprojt + tg[:, i : i + 1] * table_ref[i : i + 1, :]
    dtable_ref[...] = dtable
    dprojt_ref[...] = dprojt


def per_device(node_query, node_key, node_value, out_grad, tile_mask, tile_type, edge_table, edge_proj):
    vmem = pl.BlockSpec(memory_space=pltpu.VMEM)
    smem = pl.BlockSpec(memory_space=pltpu.SMEM)
    half = (ROWS, NZ * HD)
    proj_t = edge_proj.T
    spread = pl.pallas_call(
        kernel,
        out_shape=(
            jax.ShapeDtypeStruct((NZ, HALF, 128), BF16),
            jax.ShapeDtypeStruct((NZ, HALF, 128), BF16),
            jax.ShapeDtypeStruct((NZ, ROWS, 128), BF16),
            jax.ShapeDtypeStruct((2 * NZ, 128), F32),
        ),
        in_specs=[vmem] * 4 + [smem] * 2 + [vmem] * 2,
        out_specs=(vmem,) * 4,
        scratch_shapes=[
            pltpu.VMEM((NZ, ROWS, 128), BF16),
            pltpu.VMEM((NZ, ROWS, 128), BF16),
            pltpu.VMEM((NY, KB, 128), BF16),
            pltpu.VMEM((NXC, KB, 128), BF16),
            pltpu.VMEM((QN, 128), BF16),
            pltpu.VMEM((QN, 128), BF16),
            pltpu.VMEM((256, QN), BF16),
            pltpu.VMEM((128, QN), BF16),
            pltpu.VMEM((2, KB, 128), BF16),
            pltpu.VMEM((QN, 128), BF16),
            pltpu.VMEM((NZ, 1, 128), F32),
            pltpu.VMEM((PLANE, 1, 128), F32),
            pltpu.VMEM((16, 128), F32),
            pltpu.VMEM((16, 128), F32),
            pltpu.VMEM((128, 128), F32),
            pltpu.VMEM((2, KB, QN), F32),
            pltpu.VMEM((2, KB, QN), F32),
            pltpu.VMEM((NXC, KB, QN), BF16),
            pltpu.VMEM((NXC, KB, QN), F32),
            pltpu.VMEM((NXC, 8, QN), F32),
            pltpu.VMEM((8, QN), F32),
            pltpu.VMEM((NY, 3, 8, 128), F32),
            pltpu.VMEM((128, QN), F32),
            pltpu.VMEM((128, QN), F32),
            pltpu.VMEM((2, NZ, QN), F32),
            pltpu.VMEM((NY, HD, KB), BF16),
            pltpu.VMEM((NY, HD, KB), BF16),
            pltpu.VMEM((NY, HD, KB), BF16),
            pltpu.VMEM((NY, HD, KB), BF16),
            pltpu.VMEM((NX, KB, 128), BF16),
            pltpu.VMEM((NX, KB, 128), BF16),
            pltpu.VMEM((NX, KB, 128), BF16),
            pltpu.VMEM((NX, KB, 128), BF16),
            pltpu.VMEM((PLANE, 1, 128), F32),
            pltpu.VMEM((2 * NZ, 1, 128), F32),
            pltpu.VMEM((NZ, HALF, 128), BF16),
            pltpu.VMEM((NZ, HALF, 128), BF16),
            pltpu.VMEM((NZ, HALF, 128), BF16),
            pltpu.VMEM((NZ, HALF, 128), BF16),
            pltpu.VMEM((NZ, ROWS, 128), BF16),
            pltpu.VMEM((NZ, ROWS, 128), BF16),
            pltpu.SemaphoreType.DMA((16,)),
            pltpu.SemaphoreType.DMA((N_SEMS,)),
        ],
        compiler_params=pltpu.CompilerParams(
            collective_id=0, has_side_effects=True, vmem_limit_bytes=56 * 1024 * 1024
        ),
        cost_estimate=pl.CostEstimate(
            flops=12 * QN * NXC * KB * 128, bytes_accessed=600_000, transcendentals=QN * NXC * KB
        ),
    )(node_query, node_key, node_value, out_grad, tile_mask, tile_type, edge_table, proj_t)
    att, dq, dk, dv, dtable, dprojt = pl.pallas_call(
        lay_out,
        out_shape=(
            jax.ShapeDtypeStruct(half, BF16),
            jax.ShapeDtypeStruct(half, F32),
            jax.ShapeDtypeStruct(half, F32),
            jax.ShapeDtypeStruct(half, F32),
            jax.ShapeDtypeStruct((TYPES, 128), F32),
            jax.ShapeDtypeStruct((2 * NZ, 128), F32),
        ),
        in_specs=[vmem] * 6,
        out_specs=(vmem,) * 6,
        scratch_shapes=[pltpu.VMEM((128, 128), F32)],
    )(*spread, edge_table, proj_t)
    return att, dq, dk, dv, dtable, dprojt.T


def solution(mesh):
    split = P("grid", "head")
    return jax.shard_map(
        per_device,
        mesh=mesh,
        in_specs=(split, split, split, split, P("grid", None, None), P("grid", None, None), P(), P()),
        out_specs=(split, split, split, split, P(), P()),
        check_vma=False,
    )
```
